32 devices in a mesh: ment: 8 (over z, x), ent: 4 (over y, core).
Axes of the slice: x: 2, y: 2, z: 4, core: 2. Of those that a mesh axis runs over, the one named last changes fastest.
Arguments:
- hidden_in: bfloat16 [512, 32, 1024], P('ment'), may hold values from -6 to 6
- w_qkv: bfloat16 [1024, 3, 1024], P(None, None, 'ent'), may hold values from -0.1875 to 0.1875
- w_out: bfloat16 [1024, 1024], P('ent'), may hold values from -0.1875 to 0.1875
- ln_gain: float32 [1024], replicated, may hold values from 0.5 to 1.5
- ln_bias: float32 [1024], replicated, may hold values from -3 to 3
- table: bfloat16 [32, 256, 1024], P('ent'), may hold values from -0.5 to 0.5
- key_len: int32 [512], P('ment'), may hold values from 4 to 32
- gold_block: int32 [512], P('ment'), may hold values from 0 to 31
- gold_row: int32 [512], P('ment'), may hold values from 0 to 255
- neg_blocks: int32 [8, 4], P('ment'), may hold values from 0 to 31, as said below
Outputs:
- grad_hidden: bfloat16 [512, 32, 1024], P(('ment', 'ent'))
- grad_qkv: float32 [1024, 3, 1024], P('ment', None, 'ent')
- grad_wo: float32 [1024, 1024], P('ent', 'ment')
- grad_ln: float32 [2, 1024], P(None, 'ment')
- grad_table: float32 [32, 256, 1024], P('ent', 'ment')
The draws below stay inside these ranges and needn't reach their ends.
Inputs may be any that keep to these rules, and one draw needn't show every extreme that they name: `neg_blocks`: each row lists 4 different blocks.
All inputs are finite; a program needn't handle non-finite values.
Results may differ from the reference program's by a relative error of at most 0.028.
Values may be sent and summed in bfloat16 or wider, within the bound.
No kernel may reach another device: no remote copies, remote signals or barrier semaphores. Data moves between devices by JAX's collectives and lax.ppermute only.
A program may use at most 128 MiB of HBM per device.

```python
import jax
import jax.numpy as jnp
from jax import lax

MODEL_WIDTH = 1024
HEADS = 16
HD = 64
L = 32
MB = 64
BLK = 256
NEGB = 4
REPLICAS = 8
MENTIONS = 512
NBLK = 32


def draw_neg_blocks(key, part):
    base = jax.random.randint(key, (REPLICAS, NBLK), 0, 65536)
    heat = jax.random.randint(jax.random.fold_in(key, 7), (NBLK,), 0, 4)
    top_owner = jax.random.randint(jax.random.fold_in(key, 11), (), 0, REPLICAS)
    low_owner = jax.random.randint(jax.random.fold_in(key, 13), (), 0, REPLICAS)
    boost = jnp.zeros((REPLICAS, NBLK), jnp.int32)
    boost = boost.at[top_owner, NBLK - 1].set(4)
    boost = boost.at[low_owner, 0].set(4)
    ranked = (base + (heat[None, :] + boost) * 65536) * NBLK + jnp.arange(NBLK, dtype=jnp.int32)[None, :]
    picked = lax.top_k(ranked, NEGB)[1]
    return picked.astype(jnp.int32)


def with_ends(entries, stream_key, least, top_value):
    spot = [jax.random.randint(jax.random.fold_in(stream_key, axis), (), 0, length) for axis, length in enumerate(entries.shape)]
    longest = entries.shape.index(max(entries.shape))
    neighbour = spot[:longest] + [(spot[longest] + 1) % entries.shape[longest]] + spot[longest + 1:]
    return entries.at[tuple(spot)].set(least).at[tuple(neighbour)].set(top_value)


def with_spikes(array, rng, source, target, shards_of, factor):
    def block_of(axis_at):
        return (jnp.arange(array.shape[axis_at]) // (array.shape[axis_at] // shards_of)).reshape((-1,) + (1,) * (array.ndim - 1 - axis_at))

    one_side = jax.random.permutation(rng, shards_of)[block_of(target)]
    other_side = (block_of(target) + shards_of // 2) % shards_of
    return jnp.where((block_of(source) == one_side) | (block_of(source) == other_side), factor * array, array)


def block_levels(key, extent, shards, low, largest):
    gain = 1.0
    for position, parts in shards:
        steps = jax.random.uniform(jax.random.fold_in(jax.random.fold_in(key, 6), position), (parts,), jnp.float32, low / len(shards), largest / len(shards))
        gain = gain * jnp.repeat(jnp.exp(steps), extent[position] // parts).reshape((-1,) + (1,) * (len(extent) - 1 - position))
    return gain


def gaussian(key, shape, deviation, bound, pieces=(), kind=jnp.bfloat16):
    level = block_levels(key, shape, pieces, -0.22, 0.18) if pieces else 1.0
    entries = jax.random.normal(key, shape, jnp.float32) * deviation * level
    return jnp.minimum(jnp.maximum(entries, -bound), bound).astype(kind)


def gaussian_with(key, extent, spread, reach, pieces, heavy, kind=jnp.bfloat16):
    array = spread * jax.random.normal(key, extent, jnp.float32)
    if pieces:
        array = array * block_levels(key, extent, pieces, -0.22, 0.18)
    return jnp.clip(with_spikes(array, jax.random.fold_in(key, 3), *heavy), -reach, reach).astype(kind)


def setup_inputs(seed: int = 0) -> dict:
    splits = jax.random.split(jax.random.key(seed), 11)
    return {
        "hidden_in": gaussian_with(splits[0], (MENTIONS, L, MODEL_WIDTH), 1.0, 6.0, ((0, 8),), (0, 2, 8, 2.0)),
        "w_qkv": gaussian(splits[1], (MODEL_WIDTH, 3, MODEL_WIDTH), MODEL_WIDTH ** -0.5, 0.1875, ((2, 4),)),
        "w_out": gaussian(splits[2], (MODEL_WIDTH, MODEL_WIDTH), MODEL_WIDTH ** -0.5, 0.1875, ((0, 4),)),
        "ln_gain": jnp.clip(1.0 + 0.1 * jax.random.normal(splits[3], (MODEL_WIDTH,), jnp.float32), 0.5, 1.5),
        "ln_bias": gaussian(splits[4], (MODEL_WIDTH,), 0.5, 3.0, (), jnp.float32),
        "table": gaussian(splits[5], (NBLK, BLK, MODEL_WIDTH), (MODEL_WIDTH // 9) ** -0.5, 0.5, ((0, 4),)),
        "key_len": with_ends(jax.random.randint(splits[6], (MENTIONS,), 4, L + 1), jax.random.fold_in(splits[6], 1), 4, L).astype(jnp.int32),
        "gold_block": with_ends(jax.random.randint(splits[7], (MENTIONS,), 0, NBLK), jax.random.fold_in(splits[7], 1), 0, NBLK - 1).astype(jnp.int32),
        "gold_row": with_ends(jax.random.randint(splits[8], (MENTIONS,), 0, BLK), jax.random.fold_in(splits[8], 1), 0, BLK - 1).astype(jnp.int32),
        "neg_blocks": draw_neg_blocks(jax.random.fold_in(splits[10], 71), 0),
    }


ln_eps = 1e-06

def reference(hidden_in, w_qkv, w_out, ln_gain, ln_bias, table, key_len, gold_block, gold_row, neg_blocks):
    gradient_total = hidden_in.shape[0]
    score_scale = HD ** (-0.5)
    cls_rows = hidden_in[:, 0, :]
    query = jnp.dot(cls_rows, w_qkv[:, 0, :], preferred_element_type=jnp.float32).astype(jnp.bfloat16)
    w_keyval = w_qkv[:, 1:, :].reshape(MODEL_WIDTH, 2 * MODEL_WIDTH)
    keyval = jnp.dot(hidden_in.reshape(gradient_total * L, MODEL_WIDTH), w_keyval, preferred_element_type=jnp.float32)
    keyval = keyval.astype(jnp.bfloat16).reshape(gradient_total, L, 2, HEADS, HD)
    key_heads = keyval[:, :, 0].astype(jnp.float32)
    value_heads = keyval[:, :, 1].astype(jnp.float32)
    query_heads = query.reshape(gradient_total, HEADS, HD).astype(jnp.float32)
    attention_scores = jnp.einsum('ybn,yqbn->ybq', query_heads, key_heads) * score_scale
    valid = (jnp.arange(L, dtype=jnp.int32)[None, :] < key_len[:, None]).astype(jnp.float32)
    expo = jnp.exp(attention_scores) * valid[:, None, :]
    probs = expo / lax.optimization_barrier(jnp.sum(expo, axis=-1, keepdims=True))
    probability_half = probs.astype(jnp.bfloat16)
    context_rows = jnp.einsum('qjp,qpjb->qjb', probability_half.astype(jnp.float32), value_heads)
    context_rows = context_rows.reshape(gradient_total, MODEL_WIDTH).astype(jnp.bfloat16)
    resid = cls_rows.astype(jnp.float32) + jnp.dot(context_rows, w_out, preferred_element_type=jnp.float32)
    centre = resid - lax.optimization_barrier(jnp.mean(resid, axis=-1, keepdims=True))
    rstd = lax.rsqrt(lax.optimization_barrier(jnp.mean(centre * centre, axis=-1, keepdims=True)) + ln_eps)
    normed = centre * rstd
    embed = (normed * ln_gain + ln_bias).astype(jnp.bfloat16)
    flat_table = table.reshape(NBLK * BLK, MODEL_WIDTH)
    gold_index = (gold_block * BLK + gold_row).astype(jnp.int32)
    golds = flat_table[gold_index]
    embed_r = embed.reshape(REPLICAS, MB, MODEL_WIDTH).astype(jnp.float32)
    golds_r = golds.reshape(REPLICAS, MB, MODEL_WIDTH).astype(jnp.float32)
    inbatch = jnp.einsum('rmd,rnd->rmn', embed_r, golds_r)
    negscore = jnp.dot(embed, flat_table.T, preferred_element_type=jnp.float32)
    listed = jnp.any(neg_blocks[:, :, None] == jnp.arange(NBLK, dtype=jnp.int32)[None, None, :], axis=1)
    listed = jnp.repeat(listed.astype(jnp.float32), MB, axis=0)
    row_mask = jnp.repeat(listed, BLK, axis=1)
    norm_total = lax.optimization_barrier(jnp.sum(jnp.exp(inbatch), axis=-1)).reshape(gradient_total) + lax.optimization_barrier(jnp.sum(jnp.exp(negscore) * row_mask, axis=-1))
    lse = jnp.log(norm_total)
    eye = jnp.eye(MB, dtype=jnp.float32)
    w_inb = (jnp.exp(inbatch - lse.reshape(REPLICAS, MB, 1)) - eye[None]).astype(jnp.bfloat16)
    w_neg = (jnp.exp(negscore - lse[:, None]) * row_mask).astype(jnp.bfloat16)
    d_embed = jnp.einsum('rmn,rnd->rmd', w_inb.astype(jnp.float32), golds_r).reshape(gradient_total, MODEL_WIDTH)
    d_embed = d_embed + jnp.dot(w_neg, flat_table, preferred_element_type=jnp.float32)
    gold_terms = jnp.einsum('rmn,rmd->rnd', w_inb.astype(jnp.float32), embed_r).reshape(gradient_total, MODEL_WIDTH)
    grad_table = jnp.dot(w_neg.T, embed, preferred_element_type=jnp.float32)
    grad_table = grad_table.at[gold_index].add(gold_terms)
    grad_ln = jnp.stack([lax.optimization_barrier(jnp.sum(d_embed * normed, axis=0)), lax.optimization_barrier(jnp.sum(d_embed, axis=0))])
    upper = d_embed * ln_gain
    d_resid = rstd * (upper - lax.optimization_barrier(jnp.mean(upper, axis=-1, keepdims=True)) - normed * lax.optimization_barrier(jnp.mean(upper * normed, axis=-1, keepdims=True)))
    d_resid_bf = d_resid.astype(jnp.bfloat16)
    grad_wo = jnp.dot(context_rows.T, d_resid_bf, preferred_element_type=jnp.float32)
    d_context = jnp.dot(d_resid_bf, w_out.T, preferred_element_type=jnp.float32).astype(jnp.bfloat16)
    context_head_gradient = d_context.reshape(gradient_total, HEADS, HD).astype(jnp.float32)
    probability_gradient = jnp.einsum('ybn,yqbn->ybq', context_head_gradient, value_heads)
    score_gradient = probs * (probability_gradient - lax.optimization_barrier(jnp.sum(probs * probability_gradient, axis=-1, keepdims=True)))
    query_gradient = (jnp.einsum('qjp,qpjb->qjb', score_gradient, key_heads) * score_scale).reshape(gradient_total, MODEL_WIDTH).astype(jnp.bfloat16)
    key_gradient = jnp.einsum('ryk,ryo->rkyo', score_gradient, query_heads) * score_scale
    value_gradient = jnp.einsum('ryk,ryo->rkyo', probability_half.astype(jnp.float32), context_head_gradient)
    d_keyval = jnp.stack([key_gradient, value_gradient], axis=2).reshape(gradient_total * L, 2 * MODEL_WIDTH).astype(jnp.bfloat16)
    grad_query = jnp.dot(cls_rows.T, query_gradient, preferred_element_type=jnp.float32)
    grad_keyval = jnp.dot(hidden_in.reshape(gradient_total * L, MODEL_WIDTH).T, d_keyval, preferred_element_type=jnp.float32)
    grad_qkv = jnp.concatenate([grad_query[:, None, :], grad_keyval.reshape(MODEL_WIDTH, 2, MODEL_WIDTH)], axis=1)
    input_grad = jnp.dot(d_keyval, w_keyval.T, preferred_element_type=jnp.float32).reshape(gradient_total, L, MODEL_WIDTH)
    cls_grad = jnp.dot(query_gradient, w_qkv[:, 0, :].T, preferred_element_type=jnp.float32) + d_resid
    input_grad = input_grad.at[:, 0, :].add(cls_grad)
    return (input_grad.astype(jnp.bfloat16), grad_qkv, grad_wo, grad_ln, grad_table.reshape(NBLK, BLK, MODEL_WIDTH))
```

```python
import functools

import jax
import jax.numpy as jnp
from jax import lax
from jax.experimental import pallas as pl
from jax.experimental.pallas import tpu as pltpu
from jax.sharding import PartitionSpec as P

HD = 64
EPS = 1e-06
GROUP = 8
LOW = -1e30
BF = jnp.bfloat16
F32 = jnp.float32
VMEM = pl.BlockSpec(memory_space=pltpu.VMEM)
SMEM = pl.BlockSpec(memory_space=pltpu.SMEM)


def mm(a, b):
    return jnp.dot(a, b, preferred_element_type=F32)


def mm_nt(a, b):
    return lax.dot_general(a, b, (((1,), (1,)), ((), ())), preferred_element_type=F32)


def mm_tn(a, b):
    return lax.dot_general(a, b, (((0,), (0,)), ((), ())), preferred_element_type=F32)


def sds(shape, dtype):
    return jax.ShapeDtypeStruct(shape, dtype)


def call(body, outs, ins, scratch=(), flops=0, moved=0, limit=40):
    smem = sum(1 for x in ins if x.ndim == 1 and x.dtype == jnp.int32)
    return pl.pallas_call(
        body,
        out_shape=outs,
        in_specs=[SMEM] * smem + [VMEM] * (len(ins) - smem),
        out_specs=[VMEM] * len(outs),
        scratch_shapes=list(scratch),
        compiler_params=pltpu.CompilerParams(vmem_limit_bytes=limit * 2**20),
        cost_estimate=pl.CostEstimate(flops=flops, bytes_accessed=moved, transcendentals=0),
    )(*ins)


def head_mask(heads, cols):
    head = lax.broadcasted_iota(jnp.int32, (1, heads, 1, cols), 1)
    col = lax.broadcasted_iota(jnp.int32, (1, heads, 1, cols), 3)
    return (col // HD == head).astype(F32)


def spread_heads(rows, heads):
    count, cols = rows.shape
    split = rows.reshape(count // GROUP, 1, GROUP, cols)
    return (split * head_mask(heads, cols)).reshape(heads * count, cols).astype(BF)


def pick_heads(rows, heads):
    count, cols = rows.shape
    split = rows.reshape(count // (heads * GROUP), heads, GROUP, cols)
    return jnp.sum(split * head_mask(heads, cols), axis=1).reshape(count // heads, cols)


def forward_body(
    ids, key_len, hid, w_ref, wo_ref, attn, cls_out, ctx_out, probs_out, mix_out, qx_out, *rest
):
    pays, buf = rest[:4], rest[4]
    tokens, width = hid.shape
    cols = w_ref.shape[2]
    heads = cols // HD
    count = key_len.shape[0]
    seq = tokens // count
    span = GROUP * seq
    rows = GROUP * heads
    groups = count // GROUP
    pick = lax.broadcasted_iota(jnp.int32, (GROUP, span), 1) == seq * lax.broadcasted_iota(
        jnp.int32, (GROUP, span), 0
    )
    pick = pick.astype(F32).astype(BF)
    cls = jnp.concatenate([mm(pick, hid[g * span : (g + 1) * span, :]) for g in range(groups)], axis=0)
    cls = cls.astype(BF)
    cls_out[...] = cls
    query = mm(cls, w_ref[0]).astype(BF).astype(F32)
    qx = spread_heads(query, heads)
    qx_out[...] = qx
    buf[:, 0:width] = mm_nt(qx, w_ref[1]).astype(BF)
    col = lax.broadcasted_iota(jnp.int32, (1, span), 1)
    row_ment = lax.broadcasted_iota(jnp.int32, (rows, span), 0) % GROUP
    diag = row_ment == lax.broadcasted_iota(jnp.int32, (rows, span), 1) // seq
    for g in range(groups):
        x = hid[g * span : (g + 1) * span, :]
        here = slice(g * rows, (g + 1) * rows)
        limit = jnp.zeros((1, span), jnp.int32)
        for m in range(GROUP):
            limit = jnp.where(col // seq == m, key_len[g * GROUP + m], limit)
        live = jnp.logical_and(diag, col % seq < limit)
        score = jnp.where(live, mm_nt(buf[here, 0:width], x) * HD ** (-0.5), LOW)
        expo = jnp.exp(score - jnp.max(score, axis=1, keepdims=True))
        expo = jnp.where(live, expo, 0.0)
        probs = expo / jnp.sum(expo, axis=1, keepdims=True)
        probs_out[here, :] = probs
        half = probs.astype(BF)
        buf[here, width : width + span] = half
        mix_out[here, :] = mm(half, x).astype(BF)
    ctx = pick_heads(mm(mix_out[...], w_ref[2]), heads).astype(BF)
    ctx_out[...] = ctx
    attn[...] = mm(ctx, wo_ref[...]).astype(BF)
    share = buf.shape[0] // 4
    for k in range(4):
        pays[k][...] = buf[pl.ds(pl.multiple_of((ids[1] ^ k) * share, share), share), :]


def as_column(row):
    n = row.shape[1]
    eye = lax.broadcasted_iota(jnp.int32, (n, n), 0) == lax.broadcasted_iota(jnp.int32, (n, n), 1)
    return jnp.sum(jnp.where(eye, row.astype(F32), 0.0), axis=1, keepdims=True)


def gold_place(gold_block, gold_row, first_block, block_rows):
    return as_column((gold_block[...] - first_block) * block_rows + gold_row[...]).astype(jnp.int32)


def gold_body(ids, gold_block, gold_row, table, _, gold_out):
    blocks, block_rows, width = table.shape
    place = gold_place(gold_block, gold_row, ids[1] * blocks, block_rows)
    total = jnp.zeros(gold_out.shape, F32)
    for b in range(blocks):
        at = lax.broadcasted_iota(jnp.int32, (gold_out.shape[0], block_rows), 1) + b * block_rows
        total += mm((at == place).astype(F32).astype(BF), table[b])
    gold_out[...] = total.astype(BF)


def candidates(ids, negs, place, tile_rows, blocks, block_rows, part):
    count = place.shape[0]
    col = lax.broadcasted_iota(jnp.int32, (1, blocks * tile_rows), 1)
    block = col // tile_rows
    at = block * block_rows + part * tile_rows + col % tile_rows
    hot = (at == place).astype(F32)
    named = block + ids[1] * blocks
    listed = named == negs[0]
    for k in range(1, negs.shape[0]):
        listed = jnp.logical_or(listed, named == negs[k])
    times = listed.astype(F32) + jnp.sum(hot, axis=0, keepdims=True)
    return hot, jnp.broadcast_to(times, (count, blocks * tile_rows))


def score_body(
    ids, negs, a0, a1, a2, a3, cls, gain, bias, gold_block, gold_row, table,
    embed_out, normed_out, rstd_out, score_out, pay,
):
    blocks, block_rows, width = table.shape
    parts = score_out.shape[0]
    tile_rows = block_rows // parts
    attn = (a0[...].astype(F32) + a1[...].astype(F32)) + (a2[...].astype(F32) + a3[...].astype(F32))
    resid = cls[...].astype(F32) + attn
    centre = resid - jnp.mean(resid, axis=1, keepdims=True)
    rstd = lax.rsqrt(jnp.mean(centre * centre, axis=1, keepdims=True) + EPS)
    normed = centre * rstd
    normed_out[...] = normed
    rstd_out[...] = jnp.broadcast_to(rstd, rstd_out.shape)
    embed = (normed * gain[...] + bias[...]).astype(BF)
    embed_out[...] = embed
    place = gold_place(gold_block, gold_row, ids[1] * blocks, block_rows)
    top = jnp.full((embed.shape[0], 1), LOW, F32)
    counts = []

    def tile(d):
        start = pl.multiple_of((ids[0] ^ d) * tile_rows, tile_rows)
        return table[:, pl.ds(start, tile_rows), :].reshape(blocks * tile_rows, width)

    for d in range(parts):
        score = mm_nt(embed, tile(d))
        score_out[d] = score
        _, times = candidates(ids, negs, place, tile_rows, blocks, block_rows, ids[0] ^ d)
        top = jnp.maximum(top, jnp.max(jnp.where(times > 0, score, LOW), axis=1, keepdims=True))
        counts.append(times)
    total = jnp.zeros((embed.shape[0], 1), F32)
    mean = jnp.zeros((embed.shape[0], width), F32)
    for d in range(parts):
        times = counts[d]
        expo = jnp.where(times > 0, times * jnp.exp(jnp.minimum(score_out[d] - top, 0.0)), 0.0)
        total += jnp.sum(expo, axis=1, keepdims=True)
        mean += mm(expo.astype(BF), tile(d))
    some = total > 0
    safe = jnp.where(some, total, 1.0)
    logsum = jnp.where(some, top + jnp.log(safe), LOW)
    pay[:, 0:width] = (mean / safe).astype(BF)
    high = logsum.astype(BF).astype(F32)
    mid = (logsum - high).astype(BF).astype(F32)
    low = logsum - high - mid
    lane = lax.broadcasted_iota(jnp.int32, (embed.shape[0], 128), 1)
    stats = jnp.where(lane == 0, high, jnp.where(lane == 1, mid, jnp.where(lane == 2, low, 0.0)))
    pay[:, width : width + 128] = stats.astype(BF)


def loss_body(
    ids, negs, p0, p1, p2, p3, g0, g1, g2, g3, normed_ref, rstd_ref, gain, score, gold_block, gold_row,
    w_ref, wo_ref, mix, dv_out, own_resid, vsend, vkeep, *rest,
):
    outs, (resid_buf, wide, grad_buf) = rest[:8], rest[8:]
    width = normed_ref.shape[1]
    parts, count, tile_cols = score.shape
    blocks = 8
    tile_rows = tile_cols // blocks
    heads = w_ref.shape[2] // HD
    pays = [p0, p1, p2, p3]
    logs = [jnp.sum(p[:, width : width + 128].astype(F32), axis=1, keepdims=True) for p in pays]
    top = jnp.maximum(jnp.maximum(logs[0], logs[1]), jnp.maximum(logs[2], logs[3]))
    lse = top + jnp.log(sum(jnp.exp(v - top) for v in logs))
    golds = (g0[...].astype(F32) + g1[...].astype(F32)) + (g2[...].astype(F32) + g3[...].astype(F32))
    d_embed = sum(jnp.exp(v - lse) * p[:, 0:width].astype(F32) for v, p in zip(logs, pays)) - golds
    normed = normed_ref[...]
    first = jnp.sum(d_embed * normed, axis=0, keepdims=True)
    second = jnp.sum(d_embed, axis=0, keepdims=True)
    first_high = first.astype(BF).astype(F32)
    second_high = second.astype(BF).astype(F32)
    line = lax.broadcasted_iota(jnp.int32, (16, width), 0)
    lines = jnp.where(line == 0, first_high, 0.0)
    lines = jnp.where(line == 1, second_high, lines)
    lines = jnp.where(line == 2, first - first_high, lines)
    lines = jnp.where(line == 3, second - second_high, lines)
    upper = d_embed * gain[...]
    d_resid = rstd_ref[:, 0:1] * (
        upper
        - jnp.mean(upper, axis=1, keepdims=True)
        - normed * jnp.mean(upper * normed, axis=1, keepdims=True)
    )
    resid_buf[...] = d_resid
    share = own_resid.shape[0]
    own_resid[...] = resid_buf[pl.ds(pl.multiple_of(ids[1] * share, share), share), :]
    half = d_resid.astype(BF)
    wide[0:count, :] = half
    wide[count : count + 16, :] = lines.astype(BF)
    d_ctx = mm_nt(half, wo_ref[...]).astype(BF).astype(F32)
    dx = spread_heads(d_ctx, heads)
    dv_out[...] = mm_nt(dx, w_ref[2]).astype(BF)
    grad_buf[...] = mm_tn(mix[...], dx)
    store_parts(ids, grad_buf, vsend, vkeep, 0)
    place = gold_place(gold_block, gold_row, ids[1] * blocks, parts * tile_rows)
    step = width // parts
    for d in range(parts):
        part = ids[0] ^ d
        hot, times = candidates(ids, negs, place, tile_rows, blocks, parts * tile_rows, part)
        expo = jnp.where(times > 0, times * jnp.exp(score[d] - lse), 0.0)
        outs[d][0:count, 0:tile_cols] = (expo - hot).astype(BF)
        outs[d][count : count + 16, 0:tile_cols] = jnp.zeros((16, tile_cols), BF)
        outs[d][:, tile_cols : tile_cols + step] = wide[:, pl.ds(pl.multiple_of(part * step, step), step)]


def store_parts(ids, grad_buf, send, keep, at):
    parts = 2 * send.shape[0]
    step = grad_buf.shape[0] // parts
    cols = grad_buf.shape[1]
    for d in range(parts):
        part = grad_buf[pl.ds(pl.multiple_of((ids[0] ^ d) * step, step), step), :]
        if d % 2:
            send[d // 2, :, at : at + cols] = part.astype(BF)
        else:
            keep[d // 2, :, at : at + cols] = part


def backward_body(
    ids, hid, w_ref, probs_ref, dv, qx, cls, send, keep, *rest
):
    pays, (tbuf, buf, grad_buf, zbuf) = rest[:4], rest[4:]
    tokens, width = hid.shape
    heads = w_ref.shape[2] // HD
    count = cls.shape[0]
    seq = tokens // count
    span = GROUP * seq
    rows = GROUP * heads
    for g in range(count // GROUP):
        x = hid[g * span : (g + 1) * span, :]
        here = slice(g * rows, (g + 1) * rows)
        probs = probs_ref[here, :]
        d_probs = mm_nt(dv[here, :], x)
        d_scores = probs * (d_probs - jnp.sum(probs * d_probs, axis=1, keepdims=True))
        half = (d_scores * HD ** (-0.5)).astype(BF)
        buf[here, :] = half
        tbuf[here, :] = mm(half, x).astype(BF)
    grad_buf[...] = mm_tn(tbuf[...], qx[...])
    store_parts(ids, grad_buf, send, keep, 0)
    d_query = pick_heads(mm(tbuf[...], w_ref[1]), heads).astype(BF)
    grad_buf[...] = mm_tn(cls[...], d_query)
    store_parts(ids, grad_buf, send, keep, grad_buf.shape[1])
    zbuf[...] = mm_nt(d_query, w_ref[0]).astype(BF)
    share = buf.shape[0] // 4
    few = count // 4
    for k in range(4):
        peer = ids[1] ^ k
        mine = pl.ds(pl.multiple_of(peer * share, share), share)
        pays[k][0:share, 0:width] = dv[mine, :]
        pays[k][0:share, width : width + span] = buf[mine, :]
        pays[k][share : share + few, 0:width] = zbuf[pl.ds(pl.multiple_of(peer * few, few), few), :]
        pays[k][share : share + few, width : width + span] = jnp.zeros((few, span), BF)


def pair_body(keep, got, own, s1, s2, s3):
    own[...] = keep[0] + got[0].astype(F32)
    for k, out in ((1, s1), (2, s2), (3, s3)):
        out[...] = (keep[k] + got[k].astype(F32)).astype(BF)


def hidden_body(e0, e1, e2, e3, l0, l1, l2, l3, own_resid, out):
    early, late = (e0, e1, e2, e3), (l0, l1, l2, l3)
    mentions, seq, width = out.shape
    share = early[0].shape[0]
    groups = mentions // GROUP
    rows = share // groups
    span = GROUP * seq
    first = own_resid[...]
    for part in late:
        first = first + part[share : share + mentions, 0:width].astype(F32)
    token = lax.broadcasted_iota(jnp.int32, (GROUP, seq, width), 1)
    for g in range(groups):
        here = slice(g * rows, (g + 1) * rows)
        left = [e[here, width : width + span] for e in early] + [v[here, width : width + span] for v in late]
        right = [v[here, 0:width] for v in late] + [e[here, 0:width] for e in early]
        grad = mm_tn(jnp.concatenate(left, axis=0), jnp.concatenate(right, axis=0))
        add = first[g * GROUP : (g + 1) * GROUP, :].reshape(GROUP, 1, width)
        grad = grad.reshape(GROUP, seq, width) + jnp.where(token == 0, add, 0.0)
        out[g * GROUP : (g + 1) * GROUP] = grad.astype(BF)


def table_body(*refs):
    ids = refs[0]
    w = refs[1:9]
    mine, theirs, out = refs[9:17], refs[17], refs[18]
    blocks, tile_rows, width = out.shape
    half = width // 2
    count = mine[0].shape[0]
    left = jnp.concatenate([r[0:count, 0 : blocks * tile_rows] for r in w], axis=0)
    right = jnp.concatenate([r[:, 0:half] for r in mine], axis=0)
    side = ids[1] & 1
    grad = mm_tn(left, right).reshape(blocks, tile_rows, half)
    out[:, :, pl.ds(pl.multiple_of(side * half, half), half)] = grad
    other = mm_tn(left, theirs[...]).reshape(blocks, tile_rows, half)
    out[:, :, pl.ds(pl.multiple_of((1 - side) * half, half), half)] = other


def small_body(*refs):
    w, got, wo_out, ln_out = refs[0:8], refs[8:16], refs[16], refs[17]
    cols = wo_out.shape[0]
    step = wo_out.shape[1]
    count = got[0].shape[0]
    at = w[0].shape[1] - step
    left = jnp.concatenate([r[:, r.shape[1] - cols : r.shape[1]] for r in got], axis=0)
    right = jnp.concatenate([r[0:count, at : at + step] for r in w], axis=0)
    wo_out[...] = mm_tn(left, right)
    lines = sum(r[count : count + 16, at : at + step].astype(F32) for r in w)
    ln_out[...] = lines[0:2, :] + lines[2:4, :]


def sum_body(v0, v1, v2, v3, b0, b1, b2, b3, out):
    cols = v0.shape[1]
    out[2] = (v0[...] + v1[...].astype(F32)) + (v2[...].astype(F32) + v3[...].astype(F32))
    both = (b0[...] + b1[...].astype(F32)) + (b2[...].astype(F32) + b3[...].astype(F32))
    out[1] = both[:, 0:cols]
    out[0] = both[:, cols : 2 * cols]


def swap(x, axis, size, k):
    return lax.ppermute(x, axis, [(i, i ^ k) for i in range(size)])


def after(x, *others):
    return lax.optimization_barrier((x, *others))[0]


def on_device(
    hidden_in, w_qkv, w_out, ln_gain, ln_bias, table, key_len, gold_block, gold_row, neg_blocks
):
    count, seq, width = hidden_in.shape
    cols = w_qkv.shape[2]
    heads = cols // HD
    blocks, block_rows = table.shape[0], table.shape[1]
    ments, ents = lax.axis_size("ment"), lax.axis_size("ent")
    parts = 8
    direct = ments == parts
    mine = lax.axis_index("ment") if direct else 0
    ids = jnp.stack([jnp.int32(mine), lax.axis_index("ent").astype(jnp.int32)])
    hid = hidden_in.reshape(count * seq, width)
    w = jnp.transpose(w_qkv, (1, 0, 2))
    gain, bias = ln_gain.reshape(1, width), ln_bias.reshape(1, width)
    g_block, g_row = gold_block.reshape(1, count), gold_row.reshape(1, count)
    negs = neg_blocks.reshape(neg_blocks.shape[1])
    span = GROUP * seq
    hrows = heads * count
    share = hrows // ents

    def ent(x, k):
        return swap(x, "ent", ents, k)

    def ment(x, k):
        return swap(x, "ment", ments, k)

    attn, cls, ctx, probs, mix, qx, *early = call(
        forward_body,
        [
            sds((count, width), BF),
            sds((count, width), BF),
            sds((count, cols), BF),
            sds((hrows, span), F32),
            sds((hrows, width), BF),
            sds((hrows, cols), BF),
        ]
        + [sds((share, width + span), BF)] * 4,
        [ids, key_len, hid, w, w_out],
        [pltpu.VMEM((hrows, width + span), BF)],
        flops=10**9,
        moved=8 * 2**20,
    )
    attns = [attn] + [ent(attn, k) for k in range(1, ents)]
    gold = call(
        gold_body,
        [sds((count, width), BF)],
        [ids, g_block, g_row, table, ctx],
        flops=3 * 10**8,
        moved=4 * 2**20,
    )[0]
    embed, normed, rstd, score, pay = call(
        score_body,
        [
            sds((count, width), BF),
            sds((count, width), F32),
            sds((count, 128), F32),
            sds((parts, count, blocks * block_rows // parts), F32),
            sds((count, width + 128), BF),
        ],
        [ids, negs, *attns, cls, gain, bias, g_block, g_row, table],
        flops=6 * 10**8,
        moved=6 * 2**20,
    )
    early_got = [early[0]] + [ent(after(e, attns[2]), k) for k, e in enumerate(early) if k]
    golds = [gold] + [ent(gold, k) for k in range(1, ents)]
    pays = [pay] + [ent(pay, k) for k in range(1, ents)]
    step = width // parts
    dv, own_resid, vsend, vkeep, *tiles = call(
        loss_body,
        [
            sds((hrows, width), BF),
            sds((count // ents, width), F32),
            sds((parts // 2, step, cols), BF),
            sds((parts // 2, step, cols), F32),
        ]
        + [sds((count + 16, blocks * block_rows // parts + step), BF)] * parts,
        [ids, negs, *pays, *golds, normed, rstd, gain, score, g_block, g_row, w, w_out, mix],
        [
            pltpu.VMEM((count, width), F32),
            pltpu.VMEM((count + 16, width), BF),
            pltpu.VMEM((width, cols), F32),
        ],
        flops=3 * 10**8,
        moved=6 * 2**20,
    )
    send, keep, *late = call(
        backward_body,
        [sds((parts // 2, step, 2 * cols), BF), sds((parts // 2, step, 2 * cols), F32)]
        + [sds((share + count // ents, width + span), BF)] * 4,
        [ids, hid, w, probs, dv, qx, cls],
        [
            pltpu.VMEM((hrows, width), BF),
            pltpu.VMEM((hrows, span), BF),
            pltpu.VMEM((width, cols), F32),
            pltpu.VMEM((count, width), BF),
        ],
        flops=10**9,
        moved=8 * 2**20,
    )
    late_got = [late[0]] + [ent(v, k) for k, v in enumerate(late) if k]
    grad_hidden = call(
        hidden_body,
        [sds((count // ents, seq, width), BF)],
        [*early_got, *late_got, own_resid],
        flops=3 * 10**8,
        moved=4 * 2**20,
    )[0]
    if not direct:
        return (grad_hidden, *any_size(embed, ctx, tiles, vsend, vkeep, send, keep, blocks, block_rows))

    def scatter(sent, kept):
        got = ment(sent, 1)
        own, *sums = call(
            pair_body,
            [sds(kept.shape[1:], F32)] + [sds(kept.shape[1:], BF)] * 3,
            [kept, got],
            moved=2 * 2**20,
        )
        return [own] + [ment(s, 2 * (k + 1)) for k, s in enumerate(sums)]

    side = lax.axis_index("ent") & 1
    half = width // 2
    packed = jnp.concatenate([lax.dynamic_slice_in_dim(embed, side * half, half, 1), ctx], axis=1)
    gathered = [packed] + [ment(packed, k) for k in range(1, parts)]
    theirs = ent(jnp.concatenate([g[:, :half] for g in gathered], axis=0), 1)
    w_got = [tiles[0]] + [ment(t, k) for k, t in enumerate(tiles) if k]
    vsum = scatter(vsend, vkeep)
    bsum = scatter(send, keep)
    grad_table = call(
        table_body,
        [sds((blocks, block_rows // parts, width), F32)],
        [ids, *w_got, *gathered, theirs],
        flops=3 * 10**8,
        moved=4 * 2**20,
    )[0]
    grad_wo, grad_ln = call(
        small_body,
        [sds((cols, step), F32), sds((2, step), F32)],
        [*w_got, *gathered],
        flops=10**8,
        moved=2**20,
    )
    grad_qkv = call(sum_body, [sds((3, step, cols), F32)], [*vsum, *bsum], moved=2**20)[0]
    return (grad_hidden, jnp.transpose(grad_qkv, (1, 0, 2)), grad_wo, grad_ln, grad_table)


def any_size(embed, ctx, tiles, vsend, vkeep, send, keep, blocks, block_rows):
    ments = lax.axis_size("ment")
    count, width = embed.shape
    parts = len(tiles)
    tile_rows = block_rows // parts
    step = width // parts
    stacked = jnp.stack(tiles)
    weights = stacked[:, :count, : blocks * tile_rows].reshape(parts, count, blocks, tile_rows)
    weights = jnp.transpose(weights, (1, 2, 0, 3)).reshape(count, blocks, ments, block_rows // ments)
    weights = lax.all_to_all(jnp.transpose(weights, (2, 0, 1, 3)), "ment", 0, 0)
    embeds = lax.all_gather(embed, "ment")
    grad_table = jnp.einsum("smbr,smd->brd", weights, embeds, preferred_element_type=F32)
    resid = jnp.transpose(stacked[:, :count, blocks * tile_rows :], (1, 0, 2)).reshape(count, ments, -1)
    resid = lax.all_to_all(jnp.transpose(resid, (1, 0, 2)), "ment", 0, 0)
    ctxs = lax.all_gather(ctx, "ment")
    grad_wo = jnp.einsum("smc,smd->cd", ctxs, resid, preferred_element_type=F32)
    lines = jnp.transpose(stacked[:, count:, blocks * tile_rows :], (1, 0, 2)).reshape(16, width).astype(F32)
    grad_ln = lax.psum_scatter(lines[0:2] + lines[2:4], "ment", scatter_dimension=1, tiled=True)

    def whole(sent, kept):
        both = jnp.stack([kept, sent.astype(F32)], axis=1)
        return both.reshape(width, kept.shape[2])

    value, both = whole(vsend, vkeep), whole(send, keep)
    cols = value.shape[1]
    stack = jnp.stack([both[:, cols:], both[:, :cols], value], axis=1)
    grad_qkv = lax.psum_scatter(stack, "ment", scatter_dimension=0, tiled=True)
    return grad_qkv, grad_wo, grad_ln, grad_table


def solution(mesh):
    placed = (
        P("ment", None, None),
        P(None, None, "ent"),
        P("ent", None),
        P(),
        P(),
        P("ent", None, None),
        P("ment"),
        P("ment"),
        P("ment"),
        P("ment", None),
    )
    return jax.shard_map(
        on_device,
        mesh=mesh,
        in_specs=placed,
        out_specs=(
            P(("ment", "ent"), None, None),
            P("ment", None, "ent"),
            P("ent", "ment"),
            P(None, "ment"),
            P("ent", "ment", None),
        ),
        check_vma=False,
    )
```

```python
import functools

import jax
import jax.numpy as jnp
from jax import lax
from jax.experimental import pallas as pl
from jax.experimental.pallas import tpu as pltpu
from jax.sharding import PartitionSpec as P

HD = 64
EPS = 1e-06
GROUP = 8
LOW = -1e30
BF = jnp.bfloat16
F32 = jnp.float32
VMEM = pl.BlockSpec(memory_space=pltpu.VMEM)
SMEM = pl.BlockSpec(memory_space=pltpu.SMEM)
HBM = pl.BlockSpec(memory_space=pltpu.HBM)


def mm(a, b):
    return jnp.dot(a, b, preferred_element_type=F32)


def mm_nt(a, b):
    return lax.dot_general(a, b, (((1,), (1,)), ((), ())), preferred_element_type=F32)


def mm_tn(a, b):
    return lax.dot_general(a, b, (((0,), (0,)), ((), ())), preferred_element_type=F32)


def sds(shape, dtype):
    return jax.ShapeDtypeStruct(shape, dtype)


def call(body, outs, ins, scratch=(), flops=0, moved=0, limit=20, outside=0):
    smem = sum(1 for x in ins if x.ndim == 1 and x.dtype == jnp.int32)
    inside = len(ins) - smem - outside
    return pl.pallas_call(
        body,
        out_shape=outs,
        in_specs=[SMEM] * smem + [VMEM] * inside + [HBM] * outside,
        out_specs=[VMEM] * len(outs),
        scratch_shapes=list(scratch),
        compiler_params=pltpu.CompilerParams(vmem_limit_bytes=limit * 2**20),
        cost_estimate=pl.CostEstimate(flops=flops, bytes_accessed=moved, transcendentals=0),
    )(*ins)


def head_mask(heads, cols):
    head = lax.broadcasted_iota(jnp.int32, (1, heads, 1, cols), 1)
    col = lax.broadcasted_iota(jnp.int32, (1, heads, 1, cols), 3)
    return (col // HD == head).astype(F32)


def spread_heads(rows, heads):
    count, cols = rows.shape
    split = rows.reshape(count // GROUP, 1, GROUP, cols)
    return (split * head_mask(heads, cols)).reshape(heads * count, cols).astype(BF)


def pick_heads(rows, heads):
    count, cols = rows.shape
    split = rows.reshape(count // (heads * GROUP), heads, GROUP, cols)
    return jnp.sum(split * head_mask(heads, cols), axis=1).reshape(count // heads, cols)


def forward_body(
    key_len, hid_in, w_in, wo_in, attn, cls_out, ctx_out, probs_out, mix_out, qx_out, qk_out, fold_out,
    hid, w_ref, wo_ref, sems,
):
    tokens, width = hid.shape
    cols = w_ref.shape[2]
    heads = cols // HD
    count = key_len.shape[0]
    seq = tokens // count
    span = GROUP * seq
    rows = GROUP * heads
    groups = count // GROUP
    part = [pltpu.make_async_copy(w_in.at[0], w_ref.at[0], sems.at[groups])]
    part += [
        pltpu.make_async_copy(
            hid_in.at[pl.ds(g * span, span), :], hid.at[pl.ds(g * span, span), :], sems.at[g]
        )
        for g in range(groups)
    ]
    part += [pltpu.make_async_copy(w_in.at[k], w_ref.at[k], sems.at[groups + k]) for k in (1, 2)]
    part += [pltpu.make_async_copy(wo_in, wo_ref, sems.at[groups + 3])]
    for copy in part:
        copy.start()
    pick = lax.broadcasted_iota(jnp.int32, (GROUP, span), 1) == seq * lax.broadcasted_iota(
        jnp.int32, (GROUP, span), 0
    )
    pick = pick.astype(F32).astype(BF)
    firsts = []
    for g in range(groups):
        part[1 + g].wait()
        firsts.append(mm(pick, hid[g * span : (g + 1) * span, :]))
    cls = jnp.concatenate(firsts, axis=0).astype(BF)
    cls_out[...] = cls
    part[0].wait()
    query = mm(cls, w_ref[0]).astype(BF).astype(F32)
    qx = spread_heads(query, heads)
    qx_out[...] = qx
    part[groups + 1].wait()
    qk_out[...] = mm_nt(qx, w_ref[1]).astype(BF)
    fold = fold_matrix(span, seq, 0)
    col = lax.broadcasted_iota(jnp.int32, (1, span), 1)
    diag = diagonal(rows, span, seq)
    for g in range(groups):
        x = hid[g * span : (g + 1) * span, :]
        here = slice(g * rows, (g + 1) * rows)
        limit = jnp.zeros((1, span), jnp.int32)
        for m in range(GROUP):
            limit = jnp.where(col // seq == m, key_len[g * GROUP + m], limit)
        live = jnp.logical_and(diag, col % seq < limit)
        score = jnp.where(live, mm_nt(qk_out[here, :], x) * HD ** (-0.5), LOW)
        expo = jnp.exp(score - jnp.max(score, axis=1, keepdims=True))
        expo = jnp.where(live, expo, 0.0)
        probs = expo / jnp.sum(expo, axis=1, keepdims=True)
        probs_out[here, :] = probs
        half = probs.astype(BF)
        fold_out[here, :] = mm(half, fold).astype(BF)
        mix_out[here, :] = mm(half, x).astype(BF)
    part[groups + 2].wait()
    ctx = pick_heads(mm(mix_out[...], w_ref[2]), heads).astype(BF)
    ctx_out[...] = ctx
    part[groups + 3].wait()
    attn[...] = mm(ctx, wo_ref[...]).astype(BF)


def diagonal(rows, span, seq):
    row = lax.broadcasted_iota(jnp.int32, (rows, span), 0) % GROUP
    return row == lax.broadcasted_iota(jnp.int32, (rows, span), 1) // seq


def fold_matrix(span, seq, at):
    token = lax.broadcasted_iota(jnp.int32, (span, 128), 0) % seq
    lane = lax.broadcasted_iota(jnp.int32, (span, 128), 1)
    return (token + at == lane).astype(F32).astype(BF)


def unfold(lines, rows, span, seq, at):
    token = lax.broadcasted_iota(jnp.int32, (128, span), 1) % seq
    lane = lax.broadcasted_iota(jnp.int32, (128, span), 0)
    wide = mm(lines, (token + at == lane).astype(F32).astype(BF))
    return jnp.where(diagonal(rows, span, seq), wide, 0.0).astype(BF)


def as_column(row):
    n = row.shape[1]
    eye = lax.broadcasted_iota(jnp.int32, (n, n), 0) == lax.broadcasted_iota(jnp.int32, (n, n), 1)
    return jnp.sum(jnp.where(eye, row.astype(F32), 0.0), axis=1, keepdims=True)


def as_row(column):
    n = column.shape[0]
    eye = lax.broadcasted_iota(jnp.int32, (n, n), 0) == lax.broadcasted_iota(jnp.int32, (n, n), 1)
    return jnp.sum(jnp.where(eye, column, 0.0), axis=0, keepdims=True)


def three(x):
    high = x.astype(BF).astype(F32)
    mid = (x - high).astype(BF).astype(F32)
    return high, mid, x - high - mid


def score_body(
    ids, negs, parts, cls, gain, bias, gold_block, gold_row, table, ctx,
    embed_out, normed_out, rstd_out, pay, packed, rows_out, score_buf,
):
    blocks, block_rows, width = table.shape
    count = cls.shape[0]
    half = width // 2
    cols = ctx.shape[1]
    attn = sum(parts[k].astype(F32) for k in range(parts.shape[0]))
    resid = cls[...].astype(F32) + attn
    centre = resid - jnp.mean(resid, axis=1, keepdims=True)
    rstd = lax.rsqrt(jnp.mean(centre * centre, axis=1, keepdims=True) + EPS)
    normed = centre * rstd
    normed_out[...] = normed
    rstd_out[...] = jnp.broadcast_to(rstd, rstd_out.shape)
    embed = (normed * gain[...] + bias[...]).astype(BF)
    embed_out[...] = embed
    first = ids[1] * blocks
    g_block, g_row = as_column(gold_block[...]), as_column(gold_row[...])
    side = ids[1] & 1
    packed[:, 0:half] = embed_out[:, pl.ds(pl.multiple_of(side * half, half), half)]
    packed[:, half : half + cols] = ctx[...]
    tile_rows = rows_out.shape[1]
    rows_out[...] = table[:, pl.ds(pl.multiple_of(ids[0] * tile_rows, tile_rows), tile_rows), :]
    place = (g_block - first.astype(F32)) * block_rows + g_row
    top = jnp.full((count, 1), LOW, F32)
    counts = []
    for b in range(blocks):
        score = mm_nt(embed, table[b])
        score_buf[b] = score
        at = lax.broadcasted_iota(jnp.int32, (count, block_rows), 1) + b * block_rows
        hot = (at.astype(F32) == place).astype(F32)
        times = jnp.sum(hot, axis=0, keepdims=True)
        listed = jnp.int32(0)
        for k in range(negs.shape[0]):
            listed = jnp.where(negs[k] == first + b, 1, listed)
        times = jnp.broadcast_to(times + listed.astype(F32), (count, block_rows))
        top = jnp.maximum(top, jnp.max(jnp.where(times > 0, score, LOW), axis=1, keepdims=True))
        counts.append((times, hot))
    total = jnp.zeros((count, 1), F32)
    mean = jnp.zeros((2 * count, width), F32)
    for b in range(blocks):
        times, hot = counts[b]
        expo = jnp.where(times > 0, times * jnp.exp(jnp.minimum(score_buf[b] - top, 0.0)), 0.0)
        total += jnp.sum(expo, axis=1, keepdims=True)
        mean += mm(jnp.concatenate([expo, hot], axis=0).astype(BF), table[b])
    some = total > 0
    safe = jnp.where(some, total, 1.0)
    store_mean(pay, mean[0:count] / safe, jnp.where(some, top + jnp.log(safe), LOW))
    pay[:, width + 128 :] = mean[count:].astype(BF)


def store_mean(pay, mean, logsum):
    count, width = mean.shape
    pay[:, 0:width] = mean.astype(BF)
    high, mid, low = three(logsum)
    lane = lax.broadcasted_iota(jnp.int32, (count, 128), 1)
    stats = jnp.where(lane == 0, high, jnp.where(lane == 1, mid, jnp.where(lane == 2, low, 0.0)))
    pay[:, width : width + 128] = stats.astype(BF)


def merge_means(p, q, width):
    one, two = [jnp.sum(v[:, width : width + 128].astype(F32), axis=1, keepdims=True) for v in (p, q)]
    top = jnp.maximum(one, two)
    logsum = top + jnp.log(jnp.exp(one - top) + jnp.exp(two - top))
    mean = jnp.exp(one - logsum) * p[:, 0:width].astype(F32)
    golds = p[:, width + 128 :].astype(F32) + q[:, width + 128 :].astype(F32)
    return mean + jnp.exp(two - logsum) * q[:, 0:width].astype(F32), logsum, golds


def merge_body(p, q, out):
    width = (out.shape[1] - 128) // 2
    mean, logsum, golds = merge_means(p[...], q[...], width)
    store_mean(out, mean, logsum)
    out[:, width + 128 :] = golds.astype(BF)


def loss_body(
    ids, negs, p0, p1, normed_ref, rstd_ref, gain, w_ref, wo_ref, mix, gold_block, gold_row,
    dv_out, own_resid, vsend, vkeep, wide, resid_buf, grad_buf,
):
    count, width = normed_ref.shape
    heads = w_ref.shape[2] // HD
    mean, lse, golds = merge_means(p0[...], p1[...], width)
    d_embed = mean - golds
    normed = normed_ref[...]
    upper = d_embed * gain[...]
    d_resid = rstd_ref[:, 0:1] * (
        upper
        - jnp.mean(upper, axis=1, keepdims=True)
        - normed * jnp.mean(upper * normed, axis=1, keepdims=True)
    )
    half = d_resid.astype(BF)
    d_ctx = mm_nt(half, wo_ref[...]).astype(BF).astype(F32)
    dx = spread_heads(d_ctx, heads)
    dv_out[...] = mm_nt(dx, w_ref[2]).astype(BF)
    grad_buf[...] = mm_tn(mix[...], dx)
    store_parts(ids, grad_buf, vsend, vkeep)
    resid_buf[...] = d_resid
    share = own_resid.shape[0]
    own_resid[...] = resid_buf[pl.ds(pl.multiple_of(ids[1] * share, share), share), :]
    first = jnp.sum(d_embed * normed, axis=0, keepdims=True)
    second = jnp.sum(d_embed, axis=0, keepdims=True)
    first_high = first.astype(BF).astype(F32)
    second_high = second.astype(BF).astype(F32)
    lane = lax.broadcasted_iota(jnp.int32, (1, count), 1)
    lists = jnp.zeros((1, count), F32)
    for k in range(negs.shape[0]):
        lists = jnp.where(lane == k, negs[k].astype(F32), lists)
    logs = [*three(as_row(lse)), gold_block[...].astype(F32), gold_row[...].astype(F32), lists]
    logs = [jnp.concatenate([v] * (width // count), axis=1) for v in logs]
    line = lax.broadcasted_iota(jnp.int32, (16, width), 0)
    lines = jnp.zeros((16, width), F32)
    for k, v in enumerate(
        [first_high, second_high, first - first_high, second - second_high] + logs
    ):
        lines = jnp.where(line == k, v, lines)
    wide[0:count, :] = half
    wide[count : count + 16, :] = lines.astype(BF)


def store_parts(ids, grad_buf, send, keep):
    parts = 2 * send.shape[0]
    step = grad_buf.shape[0] // parts
    for d in range(parts):
        part = grad_buf[pl.ds(pl.multiple_of((ids[0] ^ d) * step, step), step), :]
        if d % 2:
            send[d // 2] = part.astype(BF)
        else:
            keep[d // 2] = part


def backward_body(
    ids, hid, w_ref, probs_ref, dv, qk, folded, far, near, own, tbuf, d_query_out, buf, zbuf
):
    tokens, width = hid.shape
    heads = w_ref.shape[2] // HD
    count = d_query_out.shape[0]
    seq = tokens // count
    span = GROUP * seq
    rows = GROUP * heads
    fold = fold_matrix(span, seq, seq)
    for g in range(count // GROUP):
        x = hid[g * span : (g + 1) * span, :]
        here = slice(g * rows, (g + 1) * rows)
        probs = probs_ref[here, :]
        d_probs = mm_nt(dv[here, :], x)
        d_scores = probs * (d_probs - jnp.sum(probs * d_probs, axis=1, keepdims=True))
        half = (d_scores * HD ** (-0.5)).astype(BF)
        buf[here, :] = (folded[here, :].astype(F32) + mm(half, fold)).astype(BF)
        tbuf[here, :] = mm(half, x).astype(BF)
    d_query = pick_heads(mm(tbuf[...], w_ref[1]), heads).astype(BF)
    d_query_out[...] = d_query
    zbuf[...] = mm_nt(d_query, w_ref[0]).astype(BF)
    share = dv.shape[0] // 4
    few = count // 4
    for k, out in ((0, own), (1, near), (2, far.at[0]), (3, far.at[1])):
        peer = ids[1] ^ k
        mine = pl.ds(pl.multiple_of(peer * share, share), share)
        out[0:share, 0:width] = dv[mine, :]
        out[0:share, width : 2 * width] = qk[mine, :]
        out[0:share, 2 * width :] = buf[mine, :]
        out[share : share + few, 0:width] = zbuf[pl.ds(pl.multiple_of(peer * few, few), few), :]
        out[share : share + few, width:] = jnp.zeros((few, width + 128), BF)


def spread_body(tbuf, qx, d_query, cls, wide, spread, grad_buf):
    count, width = cls.shape
    cols = qx.shape[1]
    grad_buf[...] = mm_tn(tbuf[...], qx[...])
    step = width // spread.shape[0]
    at = (step, step + count, step + 2 * count)
    for r in range(spread.shape[0]):
        here = slice(r * step, (r + 1) * step)
        spread[r, 0:step, :] = grad_buf[here, :].astype(BF)
        spread[r, at[0] : at[1], :] = d_query[...]
        spread[r, at[1] : at[2], 0:step] = cls[:, here]
        spread[r, at[1] : at[2], step : 2 * step] = wide[0:count, here]
        spread[r, at[2] :, 0:step] = wide[count:, here]
        spread[r, at[2] :, step:] = jnp.zeros((16, spread.shape[2] - step), BF)


def fold_x_body(keep, got, kept, sent):
    for k in range(2):
        kept[k] = keep[2 * k] + got[2 * k].astype(F32)
        sent[k] = (keep[2 * k + 1] + got[2 * k + 1].astype(F32)).astype(BF)


def fold_z_body(keep, got, kept, sent):
    kept[...] = keep[0] + got[0].astype(F32)
    sent[...] = (keep[1] + got[1].astype(F32)).astype(BF)


def hidden_body(p0, p1, p2, p3, own_resid, out):
    pays = (p0, p1, p2, p3)
    mentions, seq, width = out.shape
    share = p0.shape[0] - mentions
    groups = mentions // GROUP
    rows = share // groups
    span = GROUP * seq
    first = own_resid[...]
    for p in pays:
        first = first + p[share : share + mentions, 0:width].astype(F32)
    token = lax.broadcasted_iota(jnp.int32, (GROUP, seq, width), 1)
    for g in range(groups):
        here = slice(g * rows, (g + 1) * rows)
        left = [unfold(p[here, 2 * width :], rows, span, seq, 0) for p in pays]
        left += [unfold(p[here, 2 * width :], rows, span, seq, seq) for p in pays]
        right = [p[here, 0:width] for p in pays] + [p[here, width : 2 * width] for p in pays]
        grad = mm_tn(jnp.concatenate(left, axis=0), jnp.concatenate(right, axis=0))
        add = first[g * GROUP : (g + 1) * GROUP, :].reshape(GROUP, 1, width)
        grad = grad.reshape(GROUP, seq, width) + jnp.where(token == 0, add, 0.0)
        out[g * GROUP : (g + 1) * GROUP] = grad.astype(BF)


ORDER = (0, 4, 2, 6, 1, 5, 3, 7)


def table_body(listings, ids, mine_all, other_all, spread, rows_ref, out, weights):
    blocks, tile_rows, width = out.shape
    half = width // 2
    count = mine_all.shape[1]
    at = spread.shape[1] - 16
    step = width // spread.shape[0]
    tile = blocks * tile_rows
    side = ids[1] & 1
    mine = pl.ds(pl.multiple_of(side * half, half), half)
    theirs = pl.ds(pl.multiple_of((1 - side) * half, half), half)
    rows_mine = rows_ref[:, :, mine].reshape(tile, half)
    rows_theirs = rows_ref[:, :, theirs].reshape(tile, half)
    sources = [mine_all[k] for k in range(mine_all.shape[0])]
    others = [other_all[k] for k in range(mine_all.shape[0])]
    left = jnp.concatenate([s[:, 0:half] for s in sources], axis=0)
    right = jnp.concatenate([s[:, 0:half] for s in others], axis=0)
    score = mm_nt(left, rows_mine) + mm_nt(right, rows_theirs)
    col = lax.broadcasted_iota(jnp.int32, (1, tile), 1)
    block = (col // tile_rows + ids[1] * blocks).astype(F32)
    row = (col % tile_rows + ids[0] * tile_rows).astype(F32)
    for d, source in enumerate(sources):
        lines = spread[ids[0] ^ ORDER[d], at:, 0:count].astype(F32)
        lse = as_column(lines[4:5] + lines[5:6] + lines[6:7])
        hot = jnp.logical_and(as_column(lines[7:8]) == block, as_column(lines[8:9]) == row).astype(F32)
        times = jnp.sum(hot, axis=0, keepdims=True)
        listed = jnp.zeros((1, tile), F32)
        for k in range(listings):
            listed = jnp.where(lines[9:10, k : k + 1] == block, 1.0, listed)
        times = jnp.broadcast_to(times + listed, (count, tile))
        expo = jnp.exp(score[d * count : (d + 1) * count, :] - lse)
        expo = jnp.where(times > 0, times * expo, 0.0)
        weights[d * count : (d + 1) * count, :] = (expo - hot).astype(BF)
    out[:, :, mine] = mm_tn(weights[...], left).reshape(blocks, tile_rows, half)
    out[:, :, theirs] = mm_tn(weights[...], right).reshape(blocks, tile_rows, half)


def small_body(ids, gathered, spread, v0, v1, qkv_out, wo_out, ln_out):
    cols, step = wo_out.shape
    count = gathered.shape[1]
    at = gathered.shape[2] - cols
    parts = spread.shape[0]
    rows = (step, step + count, step + 2 * count)
    left = [gathered[d, :, at : at + cols] for d in range(parts)]
    right = [spread[ids[0] ^ d, rows[1] : rows[2], step : 2 * step] for d in ORDER]
    wo_out[...] = mm_tn(jnp.concatenate(left, axis=0), jnp.concatenate(right, axis=0))
    total = sum(spread[r, rows[2] :, 0:step].astype(F32) for r in range(parts))
    ln_out[...] = total[0:2, :] + total[2:4, :]
    left = [spread[r, rows[1] : rows[2], 0:step] for r in range(parts)]
    right = [spread[r, rows[0] : rows[1], :] for r in range(parts)]
    qkv_out[0] = mm_tn(jnp.concatenate(left, axis=0), jnp.concatenate(right, axis=0))
    qkv_out[1] = sum(spread[r, 0:step, :].astype(F32) for r in range(parts))
    qkv_out[2] = v0[...] + v1[...].astype(F32)


def swap(x, axis, size, k):
    return lax.ppermute(x, axis, [(i, i ^ k) for i in range(size)])


def after(x, *others):
    return lax.optimization_barrier((x, *others))[0]


def on_device(
    hidden_in, w_qkv, w_out, ln_gain, ln_bias, table, key_len, gold_block, gold_row, neg_blocks
):
    count, seq, width = hidden_in.shape
    cols = w_qkv.shape[2]
    heads = cols // HD
    blocks, block_rows = table.shape[0], table.shape[1]
    ments, ents = lax.axis_size("ment"), lax.axis_size("ent")
    parts = 8
    direct = ments == parts
    mine = lax.axis_index("ment") if direct else 0
    ids = jnp.stack([jnp.int32(mine), lax.axis_index("ent").astype(jnp.int32)])
    hid = hidden_in.reshape(count * seq, width)
    w = jnp.transpose(w_qkv, (1, 0, 2))
    gain, bias = ln_gain.reshape(1, width), ln_bias.reshape(1, width)
    g_block, g_row = gold_block.reshape(1, count), gold_row.reshape(1, count)
    negs = neg_blocks.reshape(neg_blocks.shape[1])
    span = GROUP * seq
    hrows = heads * count
    share = hrows // ents
    few = count // ents
    step = width // parts
    pairs = parts // 2

    def ent(x, k):
        return swap(x, "ent", ents, k)

    def ment(x, k):
        return swap(x, "ment", ments, k)

    attn, cls, ctx, probs, mix, qx, qk, folded = call(
        forward_body,
        [
            sds((count, width), BF),
            sds((count, width), BF),
            sds((count, cols), BF),
            sds((hrows, span), F32),
            sds((hrows, width), BF),
            sds((hrows, cols), BF),
            sds((hrows, width), BF),
            sds((hrows, 128), BF),
        ],
        [key_len, hid, w, w_out],
        [
            pltpu.VMEM(hid.shape, BF),
            pltpu.VMEM(w.shape, BF),
            pltpu.VMEM(w_out.shape, BF),
            pltpu.SemaphoreType.DMA((count // GROUP + 4,)),
        ],
        flops=10**9,
        moved=8 * 2**20,
        limit=60,
        outside=3,
    )
    attns = lax.all_gather(attn, "ent")
    embed, normed, rstd, pay, packed, table_rows = call(
        score_body,
        [
            sds((count, width), BF),
            sds((count, width), F32),
            sds((count, 128), F32),
            sds((count, 2 * width + 128), BF),
            sds((count, width // 2 + cols), BF),
            sds((blocks, block_rows // parts, width), BF),
        ],
        [ids, negs, attns, cls, gain, bias, g_block, g_row, table, ctx],
        [pltpu.VMEM((blocks, count, block_rows), F32)],
        flops=6 * 10**8,
        moved=6 * 2**20,
    )
    pay_pair = call(merge_body, [sds(pay.shape, BF)], [pay, ent(pay, 1)], moved=2**19)[0]
    pay_other = ent(pay_pair, 2)
    dv, own_resid, vsend, vkeep, wide = call(
        loss_body,
        [
            sds((hrows, width), BF),
            sds((few, width), F32),
            sds((pairs, step, cols), BF),
            sds((pairs, step, cols), F32),
            sds((count + 16, width), BF),
        ],
        [ids, negs, pay_pair, pay_other, normed, rstd, gain, w, w_out, mix, g_block, g_row],
        [pltpu.VMEM((count, width), F32), pltpu.VMEM((width, cols), F32)],
        flops=3 * 10**8,
        moved=6 * 2**20,
    )
    far, near, own, mixed, d_query = call(
        backward_body,
        [
            sds((2, share + few, 2 * width + 128), BF),
            sds((share + few, 2 * width + 128), BF),
            sds((share + few, 2 * width + 128), BF),
            sds((hrows, width), BF),
            sds((count, cols), BF),
        ],
        [ids, hid, w, probs, dv, qk, folded],
        [pltpu.VMEM((hrows, 128), BF), pltpu.VMEM((count, width), BF)],
        flops=10**9,
        moved=8 * 2**20,
    )
    spread = call(
        spread_body,
        [sds((parts, step + 2 * count + 16, cols), BF)],
        [mixed, qx, d_query, cls, wide],
        [pltpu.VMEM((width, cols), F32)],
        flops=10**8,
        moved=3 * 2**20,
    )[0]
    far_got = ent(far, 2)
    pays = [own, ent(near, 1), far_got[0], ent(far_got[1], 1)]
    grad_hidden = call(
        hidden_body,
        [sds((few, seq, width), BF)],
        [*pays, own_resid],
        flops=3 * 10**8,
        moved=4 * 2**20,
    )[0]
    if not direct:
        others = any_size(embed, ctx, spread, vsend, vkeep, wide, table, g_block, g_row, negs)
        return (grad_hidden, *others)

    packed = after(packed, pay_pair)
    zs = jnp.stack([packed, ment(packed, 4)])
    zs = jnp.concatenate([zs, ment(zs, 2)], axis=0)
    tile = (step, cols)
    v_keep, v_sent = call(
        fold_x_body, [sds((2, *tile), F32), sds((2, *tile), BF)], [vkeep, ment(vsend, 1)], moved=2**20
    )
    v_keep, v_send = call(
        fold_z_body, [sds(tile, F32), sds(tile, BF)], [v_keep, ment(v_sent, 2)], moved=2**19
    )
    v_got = ment(v_send, 4)
    gathered = jnp.concatenate([after(zs, v_keep), ment(zs, 1)], axis=0)
    gathered_other = ent(gathered, 1)
    spread = lax.all_to_all(after(spread, v_sent, zs), "ment", 0, 0)
    grad_table = call(
        functools.partial(table_body, negs.shape[0]),
        [sds((blocks, block_rows // parts, width), F32)],
        [ids, gathered, gathered_other, spread, table_rows],
        [pltpu.VMEM((parts * count, blocks * block_rows // parts), BF)],
        flops=5 * 10**8,
        moved=4 * 2**20,
    )[0]
    grad_qkv, grad_wo, grad_ln = call(
        small_body,
        [sds((3, *tile), F32), sds((cols, step), F32), sds((2, step), F32)],
        [ids, gathered, spread, v_keep, v_got],
        flops=10**8,
        moved=2**20,
    )
    return (grad_hidden, jnp.transpose(grad_qkv, (1, 0, 2)), grad_wo, grad_ln, grad_table)


def any_size(embed, ctx, spread, vsend, vkeep, wide, table, g_block, g_row, negs):
    ments = lax.axis_size("ment")
    count, width = embed.shape
    blocks, block_rows = table.shape[0], table.shape[1]
    few_rows = block_rows // ments
    step = width // spread.shape[0]
    sums = wide[count:].astype(F32)
    lse = lax.all_gather(sums[4, :count] + sums[5, :count] + sums[6, :count], "ment")
    blocks_of = lax.all_gather(g_block[0], "ment")
    rows_of = lax.all_gather(g_row[0], "ment")
    lists = lax.all_gather(negs, "ment")
    embeds = lax.all_gather(embed, "ment")
    at = lax.axis_index("ment") * few_rows
    rows = lax.dynamic_slice_in_dim(table, at, few_rows, 1)
    score = jnp.einsum("smd,brd->smbr", embeds, rows, preferred_element_type=F32)
    block = lax.axis_index("ent") * blocks + jnp.arange(blocks, dtype=jnp.int32)
    row = at + jnp.arange(few_rows, dtype=jnp.int32)
    hot = (blocks_of[:, :, None, None] == block[:, None]) & (rows_of[:, :, None, None] == row)
    hot = hot.astype(F32)
    listed = jnp.any(lists[:, :, None] == block, axis=1).astype(F32)
    times = (jnp.sum(hot, axis=1) + listed[:, :, None])[:, None]
    expo = jnp.where(times > 0, times * jnp.exp(score - lse[:, :, None, None]), 0.0)
    grad_table = jnp.einsum("smbr,smd->brd", (expo - hot).astype(BF), embeds, preferred_element_type=F32)
    resid = wide[:count].reshape(count, ments, -1)
    resid = lax.all_to_all(jnp.transpose(resid, (1, 0, 2)), "ment", 0, 0)
    ctxs = lax.all_gather(ctx, "ment")
    grad_wo = jnp.einsum("smc,smd->cd", ctxs, resid, preferred_element_type=F32)
    grad_ln = lax.psum_scatter(sums[0:2] + sums[2:4], "ment", scatter_dimension=1, tiled=True)
    keys = spread[:, :step].astype(F32).reshape(width, -1)
    d_query = spread[0, step : step + count]
    cls = jnp.transpose(spread[:, step + count : step + 2 * count, :step], (1, 0, 2)).reshape(count, width)
    values = jnp.stack([vkeep, vsend.astype(F32)], axis=1).reshape(width, -1)
    whole = jnp.stack([mm_tn(cls, d_query), keys, values], axis=1)
    grad_qkv = lax.psum_scatter(whole, "ment", scatter_dimension=0, tiled=True)
    return grad_qkv, grad_wo, grad_ln, grad_table


def solution(mesh):
    placed = (
        P("ment", None, None),
        P(None, None, "ent"),
        P("ent", None),
        P(),
        P(),
        P("ent", None, None),
        P("ment"),
        P("ment"),
        P("ment"),
        P("ment", None),
    )
    return jax.shard_map(
        on_device,
        mesh=mesh,
        in_specs=placed,
        out_specs=(
            P(("ment", "ent"), None, None),
            P("ment", None, "ent"),
            P("ent", "ment"),
            P(None, "ment"),
            P("ent", "ment", None),
        ),
        check_vma=False,
    )
```

```python
import functools

import jax
import jax.numpy as jnp
from jax import lax
from jax.experimental import pallas as pl
from jax.experimental.pallas import tpu as pltpu
from jax.sharding import PartitionSpec as P

HD = 64
EPS = 1e-06
GROUP = 8
LOW = -1e30
BF = jnp.bfloat16
F32 = jnp.float32
VMEM = pl.BlockSpec(memory_space=pltpu.VMEM)
SMEM = pl.BlockSpec(memory_space=pltpu.SMEM)
HBM = pl.BlockSpec(memory_space=pltpu.HBM)


def mm(a, b):
    return jnp.dot(a, b, preferred_element_type=F32)


def mm_nt(a, b):
    return lax.dot_general(a, b, (((1,), (1,)), ((), ())), preferred_element_type=F32)


def mm_tn(a, b):
    return lax.dot_general(a, b, (((0,), (0,)), ((), ())), preferred_element_type=F32)


def sds(shape, dtype):
    return jax.ShapeDtypeStruct(shape, dtype)


def call(body, outs, ins, scratch=(), flops=0, moved=0, limit=20, outside=0):
    smem = sum(1 for x in ins if x.ndim == 1 and x.dtype == jnp.int32)
    inside = len(ins) - smem - outside
    return pl.pallas_call(
        body,
        out_shape=outs,
        in_specs=[SMEM] * smem + [VMEM] * inside + [HBM] * outside,
        out_specs=[VMEM] * len(outs),
        scratch_shapes=list(scratch),
        compiler_params=pltpu.CompilerParams(vmem_limit_bytes=limit * 2**20),
        cost_estimate=pl.CostEstimate(flops=flops, bytes_accessed=moved, transcendentals=0),
    )(*ins)


def head_mask(heads, cols):
    head = lax.broadcasted_iota(jnp.int32, (1, heads, 1, cols), 1)
    col = lax.broadcasted_iota(jnp.int32, (1, heads, 1, cols), 3)
    return (col // HD == head).astype(F32)


def spread_heads(rows, heads):
    count, cols = rows.shape
    split = rows.reshape(count // GROUP, 1, GROUP, cols)
    return (split * head_mask(heads, cols)).reshape(heads * count, cols).astype(BF)


def pick_heads(rows, heads):
    count, cols = rows.shape
    split = rows.reshape(count // (heads * GROUP), heads, GROUP, cols)
    return jnp.sum(split * head_mask(heads, cols), axis=1).reshape(count // heads, cols)


def forward_body(
    key_len, hid_in, w_in, wo_in, attn, cls_out, ctx_out, probs_out, mix_out, qx_out, qk_out, fold_out,
    hid, w_ref, wo_ref, sems,
):
    tokens, width = hid.shape
    cols = w_ref.shape[2]
    heads = cols // HD
    count = key_len.shape[0]
    seq = tokens // count
    span = GROUP * seq
    rows = GROUP * heads
    groups = count // GROUP
    part = [pltpu.make_async_copy(w_in.at[0], w_ref.at[0], sems.at[groups])]
    part += [
        pltpu.make_async_copy(
            hid_in.at[pl.ds(g * span, span), :], hid.at[pl.ds(g * span, span), :], sems.at[g]
        )
        for g in range(groups)
    ]
    part += [pltpu.make_async_copy(w_in.at[k], w_ref.at[k], sems.at[groups + k]) for k in (1, 2)]
    part += [pltpu.make_async_copy(wo_in, wo_ref, sems.at[groups + 3])]
    for copy in part:
        copy.start()
    pick = lax.broadcasted_iota(jnp.int32, (GROUP, span), 1) == seq * lax.broadcasted_iota(
        jnp.int32, (GROUP, span), 0
    )
    pick = pick.astype(F32).astype(BF)
    firsts = []
    for g in range(groups):
        part[1 + g].wait()
        firsts.append(mm(pick, hid[g * span : (g + 1) * span, :]))
    cls = jnp.concatenate(firsts, axis=0).astype(BF)
    cls_out[...] = cls
    part[0].wait()
    query = mm(cls, w_ref[0]).astype(BF).astype(F32)
    qx = spread_heads(query, heads)
    qx_out[...] = qx
    part[groups + 1].wait()
    qk_out[...] = mm_nt(qx, w_ref[1]).astype(BF)
    score = []
    live = []
    col = lax.broadcasted_iota(jnp.int32, (1, span), 1)
    diag = diagonal(rows, span, seq)
    for g in range(groups):
        here = slice(g * rows, (g + 1) * rows)
        score.append(mm_nt(qk_out[here, :], hid[g * span : (g + 1) * span, :]))
        limit = jnp.zeros((1, span), jnp.int32)
        for m in range(GROUP):
            limit = jnp.where(col // seq == m, key_len[g * GROUP + m], limit)
        live.append(jnp.logical_and(diag, col % seq < limit).astype(F32))
    live = jnp.concatenate(live, axis=0) > 0
    score = jnp.where(live, jnp.concatenate(score, axis=0) * HD ** (-0.5), LOW)
    expo = jnp.exp(score - jnp.max(score, axis=1, keepdims=True))
    expo = jnp.where(live, expo, 0.0)
    probs = expo / jnp.sum(expo, axis=1, keepdims=True)
    probs_out[...] = probs
    half = probs.astype(BF)
    for g in range(groups):
        here = slice(g * rows, (g + 1) * rows)
        mix_out[here, :] = mm(half[here, :], hid[g * span : (g + 1) * span, :]).astype(BF)
    fold_out[...] = mm(half, fold_matrix(span, seq, 0)).astype(BF)
    part[groups + 2].wait()
    ctx = pick_heads(mm(mix_out[...], w_ref[2]), heads).astype(BF)
    ctx_out[...] = ctx
    part[groups + 3].wait()
    attn[...] = mm(ctx, wo_ref[...]).astype(BF)


def diagonal(rows, span, seq):
    row = lax.broadcasted_iota(jnp.int32, (rows, span), 0) % GROUP
    return row == lax.broadcasted_iota(jnp.int32, (rows, span), 1) // seq


def fold_matrix(span, seq, at):
    token = lax.broadcasted_iota(jnp.int32, (span, 128), 0) % seq
    lane = lax.broadcasted_iota(jnp.int32, (span, 128), 1)
    return (token + at == lane).astype(F32).astype(BF)


def unfold(lines, rows, span, seq, at):
    token = lax.broadcasted_iota(jnp.int32, (128, span), 1) % seq
    lane = lax.broadcasted_iota(jnp.int32, (128, span), 0)
    wide = mm(lines, (token + at == lane).astype(F32).astype(BF))
    return jnp.where(diagonal(rows, span, seq), wide, 0.0).astype(BF)


def as_column(row):
    n = row.shape[1]
    eye = lax.broadcasted_iota(jnp.int32, (n, n), 0) == lax.broadcasted_iota(jnp.int32, (n, n), 1)
    return jnp.sum(jnp.where(eye, row.astype(F32), 0.0), axis=1, keepdims=True)


def as_row(column):
    n = column.shape[0]
    eye = lax.broadcasted_iota(jnp.int32, (n, n), 0) == lax.broadcasted_iota(jnp.int32, (n, n), 1)
    return jnp.sum(jnp.where(eye, column, 0.0), axis=0, keepdims=True)


def three(x):
    high = x.astype(BF).astype(F32)
    mid = (x - high).astype(BF).astype(F32)
    return high, mid, x - high - mid


def score_body(
    ids, negs, parts, cls, gain, bias, gold_block, gold_row, table, ctx,
    embed_out, normed_out, rstd_out, pay, packed, rows_out, score_buf,
):
    blocks, block_rows, width = table.shape
    count = cls.shape[0]
    half = width // 2
    cols = ctx.shape[1]
    attn = sum(parts[k].astype(F32) for k in range(parts.shape[0]))
    resid = cls[...].astype(F32) + attn
    centre = resid - jnp.mean(resid, axis=1, keepdims=True)
    rstd = lax.rsqrt(jnp.mean(centre * centre, axis=1, keepdims=True) + EPS)
    normed = centre * rstd
    normed_out[...] = normed
    rstd_out[...] = jnp.broadcast_to(rstd, rstd_out.shape)
    embed = (normed * gain[...] + bias[...]).astype(BF)
    embed_out[...] = embed
    first = ids[1] * blocks
    g_block, g_row = as_column(gold_block[...]), as_column(gold_row[...])
    side = ids[1] & 1
    packed[:, 0:half] = embed_out[:, pl.ds(pl.multiple_of(side * half, half), half)]
    packed[:, half : half + cols] = ctx[...]
    tile_rows = rows_out.shape[1]
    rows_out[...] = table[:, pl.ds(pl.multiple_of(ids[0] * tile_rows, tile_rows), tile_rows), :]
    place = (g_block - first.astype(F32)) * block_rows + g_row
    top = jnp.full((count, 1), LOW, F32)
    counts = []
    for b in range(blocks):
        score = mm_nt(embed, table[b])
        score_buf[b] = score
        at = lax.broadcasted_iota(jnp.int32, (count, block_rows), 1) + b * block_rows
        hot = (at.astype(F32) == place).astype(F32)
        times = jnp.sum(hot, axis=0, keepdims=True)
        listed = jnp.int32(0)
        for k in range(negs.shape[0]):
            listed = jnp.where(negs[k] == first + b, 1, listed)
        times = jnp.broadcast_to(times + listed.astype(F32), (count, block_rows))
        top = jnp.maximum(top, jnp.max(jnp.where(times > 0, score, LOW), axis=1, keepdims=True))
        counts.append((times, hot))
    total = jnp.zeros((count, 1), F32)
    mean = jnp.zeros((2 * count, width), F32)
    for b in range(blocks):
        times, hot = counts[b]
        expo = jnp.where(times > 0, times * jnp.exp(jnp.minimum(score_buf[b] - top, 0.0)), 0.0)
        total += jnp.sum(expo, axis=1, keepdims=True)
        mean += mm(jnp.concatenate([expo, hot], axis=0).astype(BF), table[b])
    some = total > 0
    safe = jnp.where(some, total, 1.0)
    store_mean(pay, mean[0:count] / safe, jnp.where(some, top + jnp.log(safe), LOW))
    pay[:, width + 128 :] = mean[count:].astype(BF)


def store_mean(pay, mean, logsum):
    count, width = mean.shape
    pay[:, 0:width] = mean.astype(BF)
    high, mid, low = three(logsum)
    lane = lax.broadcasted_iota(jnp.int32, (count, 128), 1)
    stats = jnp.where(lane == 0, high, jnp.where(lane == 1, mid, jnp.where(lane == 2, low, 0.0)))
    pay[:, width : width + 128] = stats.astype(BF)


def merge_means(p, q, width):
    one, two = [jnp.sum(v[:, width : width + 128].astype(F32), axis=1, keepdims=True) for v in (p, q)]
    top = jnp.maximum(one, two)
    logsum = top + jnp.log(jnp.exp(one - top) + jnp.exp(two - top))
    mean = jnp.exp(one - logsum) * p[:, 0:width].astype(F32)
    golds = p[:, width + 128 :].astype(F32) + q[:, width + 128 :].astype(F32)
    return mean + jnp.exp(two - logsum) * q[:, 0:width].astype(F32), logsum, golds


def merge_body(p, q, out):
    width = (out.shape[1] - 128) // 2
    mean, logsum, golds = merge_means(p[...], q[...], width)
    store_mean(out, mean, logsum)
    out[:, width + 128 :] = golds.astype(BF)


def loss_body(
    ids, negs, p0, p1, normed_ref, rstd_ref, gain, w_ref, wo_ref, mix, gold_block, gold_row,
    dv_out, own_resid, vsend, vkeep, wide, resid_buf, grad_buf,
):
    count, width = normed_ref.shape
    heads = w_ref.shape[2] // HD
    mean, lse, golds = merge_means(p0[...], p1[...], width)
    d_embed = mean - golds
    normed = normed_ref[...]
    upper = d_embed * gain[...]
    d_resid = rstd_ref[:, 0:1] * (
        upper
        - jnp.mean(upper, axis=1, keepdims=True)
        - normed * jnp.mean(upper * normed, axis=1, keepdims=True)
    )
    half = d_resid.astype(BF)
    d_ctx = mm_nt(half, wo_ref[...]).astype(BF).astype(F32)
    dx = spread_heads(d_ctx, heads)
    dv_out[...] = mm_nt(dx, w_ref[2]).astype(BF)
    grad_buf[...] = mm_tn(mix[...], dx)
    store_parts(ids, grad_buf, vsend, vkeep)
    resid_buf[...] = d_resid
    share = own_resid.shape[0]
    own_resid[...] = resid_buf[pl.ds(pl.multiple_of(ids[1] * share, share), share), :]
    first = jnp.sum(d_embed * normed, axis=0, keepdims=True)
    second = jnp.sum(d_embed, axis=0, keepdims=True)
    first_high = first.astype(BF).astype(F32)
    second_high = second.astype(BF).astype(F32)
    lane = lax.broadcasted_iota(jnp.int32, (1, count), 1)
    lists = jnp.zeros((1, count), F32)
    for k in range(negs.shape[0]):
        lists = jnp.where(lane == k, negs[k].astype(F32), lists)
    logs = [*three(as_row(lse)), gold_block[...].astype(F32), gold_row[...].astype(F32), lists]
    logs = [jnp.concatenate([v] * (width // count), axis=1) for v in logs]
    line = lax.broadcasted_iota(jnp.int32, (16, width), 0)
    lines = jnp.zeros((16, width), F32)
    for k, v in enumerate(
        [first_high, second_high, first - first_high, second - second_high] + logs
    ):
        lines = jnp.where(line == k, v, lines)
    wide[0:count, :] = half
    wide[count : count + 16, :] = lines.astype(BF)


def store_parts(ids, grad_buf, send, keep):
    parts = 2 * send.shape[0]
    step = grad_buf.shape[0] // parts
    for d in range(parts):
        part = grad_buf[pl.ds(pl.multiple_of((ids[0] ^ d) * step, step), step), :]
        if d % 2:
            send[d // 2] = part.astype(BF)
        else:
            keep[d // 2] = part


def backward_body(
    ids, hid, w_ref, probs_ref, dv, qk, folded, far, near, own, tbuf, d_query_out, buf, zbuf
):
    tokens, width = hid.shape
    heads = w_ref.shape[2] // HD
    count = d_query_out.shape[0]
    seq = tokens // count
    span = GROUP * seq
    rows = GROUP * heads
    xs = [hid[g * span : (g + 1) * span, :] for g in range(count // GROUP)]
    d_probs = [mm_nt(dv[g * rows : (g + 1) * rows, :], x) for g, x in enumerate(xs)]
    d_probs = jnp.concatenate(d_probs, axis=0)
    probs = probs_ref[...]
    d_scores = probs * (d_probs - jnp.sum(probs * d_probs, axis=1, keepdims=True))
    half = (d_scores * HD ** (-0.5)).astype(BF)
    for g, x in enumerate(xs):
        here = slice(g * rows, (g + 1) * rows)
        tbuf[here, :] = mm(half[here, :], x).astype(BF)
    buf[...] = (folded[...].astype(F32) + mm(half, fold_matrix(span, seq, seq))).astype(BF)
    d_query = pick_heads(mm(tbuf[...], w_ref[1]), heads).astype(BF)
    d_query_out[...] = d_query
    zbuf[...] = mm_nt(d_query, w_ref[0]).astype(BF)
    share = dv.shape[0] // 4
    few = count // 4
    for k, out in ((0, own), (1, near), (2, far.at[0]), (3, far.at[1])):
        peer = ids[1] ^ k
        mine = pl.ds(pl.multiple_of(peer * share, share), share)
        out[0:share, 0:width] = dv[mine, :]
        out[0:share, width : 2 * width] = qk[mine, :]
        out[0:share, 2 * width :] = buf[mine, :]
        out[share : share + few, 0:width] = zbuf[pl.ds(pl.multiple_of(peer * few, few), few), :]
        out[share : share + few, width:] = jnp.zeros((few, width + 128), BF)


def spread_body(tbuf, qx, d_query, cls, wide, spread, grad_buf):
    count, width = cls.shape
    cols = qx.shape[1]
    grad_buf[...] = mm_tn(tbuf[...], qx[...])
    step = width // spread.shape[0]
    at = (step, step + count, step + 2 * count)
    for r in range(spread.shape[0]):
        here = slice(r * step, (r + 1) * step)
        spread[r, 0:step, :] = grad_buf[here, :].astype(BF)
        spread[r, at[0] : at[1], :] = d_query[...]
        spread[r, at[1] : at[2], 0:step] = cls[:, here]
        spread[r, at[1] : at[2], step : 2 * step] = wide[0:count, here]
        spread[r, at[2] :, 0:step] = wide[count:, here]
        spread[r, at[2] :, step:] = jnp.zeros((16, spread.shape[2] - step), BF)


def fold_x_body(keep, got, kept, sent):
    for k in range(2):
        kept[k] = keep[2 * k] + got[2 * k].astype(F32)
        sent[k] = (keep[2 * k + 1] + got[2 * k + 1].astype(F32)).astype(BF)


def fold_z_body(keep, got, kept, sent):
    kept[...] = keep[0] + got[0].astype(F32)
    sent[...] = (keep[1] + got[1].astype(F32)).astype(BF)


def hidden_body(p0, p1, p2, p3, own_resid, out):
    pays = (p0, p1, p2, p3)
    mentions, seq, width = out.shape
    share = p0.shape[0] - mentions
    groups = mentions // GROUP
    rows = share // groups
    span = GROUP * seq
    first = own_resid[...]
    for p in pays:
        first = first + p[share : share + mentions, 0:width].astype(F32)
    token = lax.broadcasted_iota(jnp.int32, (GROUP, seq, width), 1)
    for g in range(groups):
        here = slice(g * rows, (g + 1) * rows)
        left = [unfold(p[here, 2 * width :], rows, span, seq, 0) for p in pays]
        left += [unfold(p[here, 2 * width :], rows, span, seq, seq) for p in pays]
        right = [p[here, 0:width] for p in pays] + [p[here, width : 2 * width] for p in pays]
        grad = mm_tn(jnp.concatenate(left, axis=0), jnp.concatenate(right, axis=0))
        add = first[g * GROUP : (g + 1) * GROUP, :].reshape(GROUP, 1, width)
        grad = grad.reshape(GROUP, seq, width) + jnp.where(token == 0, add, 0.0)
        out[g * GROUP : (g + 1) * GROUP] = grad.astype(BF)


ORDER = (0, 4, 2, 6, 1, 5, 3, 7)


def table_body(listings, ids, mine_all, other_all, spread, rows_ref, out, weights):
    blocks, tile_rows, width = out.shape
    half = width // 2
    count = mine_all.shape[1]
    at = spread.shape[1] - 16
    step = width // spread.shape[0]
    tile = blocks * tile_rows
    side = ids[1] & 1
    mine = pl.ds(pl.multiple_of(side * half, half), half)
    theirs = pl.ds(pl.multiple_of((1 - side) * half, half), half)
    rows_mine = rows_ref[:, :, mine].reshape(tile, half)
    rows_theirs = rows_ref[:, :, theirs].reshape(tile, half)
    sources = [mine_all[k] for k in range(mine_all.shape[0])]
    others = [other_all[k] for k in range(mine_all.shape[0])]
    left = jnp.concatenate([s[:, 0:half] for s in sources], axis=0)
    right = jnp.concatenate([s[:, 0:half] for s in others], axis=0)
    score = mm_nt(left, rows_mine) + mm_nt(right, rows_theirs)
    col = lax.broadcasted_iota(jnp.int32, (1, tile), 1)
    block = (col // tile_rows + ids[1] * blocks).astype(F32)
    row = (col % tile_rows + ids[0] * tile_rows).astype(F32)
    for d, source in enumerate(sources):
        lines = spread[ids[0] ^ ORDER[d], at:, 0:count].astype(F32)
        lse = as_column(lines[4:5] + lines[5:6] + lines[6:7])
        hot = jnp.logical_and(as_column(lines[7:8]) == block, as_column(lines[8:9]) == row).astype(F32)
        times = jnp.sum(hot, axis=0, keepdims=True)
        listed = jnp.zeros((1, tile), F32)
        for k in range(listings):
            listed = jnp.where(lines[9:10, k : k + 1] == block, 1.0, listed)
        times = jnp.broadcast_to(times + listed, (count, tile))
        expo = jnp.exp(score[d * count : (d + 1) * count, :] - lse)
        expo = jnp.where(times > 0, times * expo, 0.0)
        weights[d * count : (d + 1) * count, :] = (expo - hot).astype(BF)
    out[:, :, mine] = mm_tn(weights[...], left).reshape(blocks, tile_rows, half)
    out[:, :, theirs] = mm_tn(weights[...], right).reshape(blocks, tile_rows, half)


def small_body(ids, gathered, spread, v0, v1, qkv_out, wo_out, ln_out):
    cols, step = wo_out.shape
    count = gathered.shape[1]
    at = gathered.shape[2] - cols
    parts = spread.shape[0]
    rows = (step, step + count, step + 2 * count)
    left = [gathered[d, :, at : at + cols] for d in range(parts)]
    right = [spread[ids[0] ^ d, rows[1] : rows[2], step : 2 * step] for d in ORDER]
    wo_out[...] = mm_tn(jnp.concatenate(left, axis=0), jnp.concatenate(right, axis=0))
    total = sum(spread[r, rows[2] :, 0:step].astype(F32) for r in range(parts))
    ln_out[...] = total[0:2, :] + total[2:4, :]
    left = [spread[r, rows[1] : rows[2], 0:step] for r in range(parts)]
    right = [spread[r, rows[0] : rows[1], :] for r in range(parts)]
    qkv_out[0] = mm_tn(jnp.concatenate(left, axis=0), jnp.concatenate(right, axis=0))
    qkv_out[1] = sum(spread[r, 0:step, :].astype(F32) for r in range(parts))
    qkv_out[2] = v0[...] + v1[...].astype(F32)


def swap(x, axis, size, k):
    return lax.ppermute(x, axis, [(i, i ^ k) for i in range(size)])


def after(x, *others):
    return lax.optimization_barrier((x, *others))[0]


def on_device(
    hidden_in, w_qkv, w_out, ln_gain, ln_bias, table, key_len, gold_block, gold_row, neg_blocks
):
    count, seq, width = hidden_in.shape
    cols = w_qkv.shape[2]
    heads = cols // HD
    blocks, block_rows = table.shape[0], table.shape[1]
    ments, ents = lax.axis_size("ment"), lax.axis_size("ent")
    parts = 8
    direct = ments == parts
    mine = lax.axis_index("ment") if direct else 0
    ids = jnp.stack([jnp.int32(mine), lax.axis_index("ent").astype(jnp.int32)])
    hid = hidden_in.reshape(count * seq, width)
    w = jnp.transpose(w_qkv, (1, 0, 2))
    gain, bias = ln_gain.reshape(1, width), ln_bias.reshape(1, width)
    g_block, g_row = gold_block.reshape(1, count), gold_row.reshape(1, count)
    negs = neg_blocks.reshape(neg_blocks.shape[1])
    span = GROUP * seq
    hrows = heads * count
    share = hrows // ents
    few = count // ents
    step = width // parts
    pairs = parts // 2

    def ent(x, k):
        return swap(x, "ent", ents, k)

    def ment(x, k):
        return swap(x, "ment", ments, k)

    attn, cls, ctx, probs, mix, qx, qk, folded = call(
        forward_body,
        [
            sds((count, width), BF),
            sds((count, width), BF),
            sds((count, cols), BF),
            sds((hrows, span), F32),
            sds((hrows, width), BF),
            sds((hrows, cols), BF),
            sds((hrows, width), BF),
            sds((hrows, 128), BF),
        ],
        [key_len, hid, w, w_out],
        [
            pltpu.VMEM(hid.shape, BF),
            pltpu.VMEM(w.shape, BF),
            pltpu.VMEM(w_out.shape, BF),
            pltpu.SemaphoreType.DMA((count // GROUP + 4,)),
        ],
        flops=10**9,
        moved=8 * 2**20,
        limit=52,
        outside=3,
    )
    attns = lax.all_gather(attn, "ent")
    embed, normed, rstd, pay, packed, table_rows = call(
        score_body,
        [
            sds((count, width), BF),
            sds((count, width), F32),
            sds((count, 128), F32),
            sds((count, 2 * width + 128), BF),
            sds((count, width // 2 + cols), BF),
            sds((blocks, block_rows // parts, width), BF),
        ],
        [ids, negs, attns, cls, gain, bias, g_block, g_row, table, ctx],
        [pltpu.VMEM((blocks, count, block_rows), F32)],
        flops=6 * 10**8,
        moved=6 * 2**20,
    )
    pay_pair = call(merge_body, [sds(pay.shape, BF)], [pay, ent(pay, 1)], moved=2**19)[0]
    pay_other = ent(pay_pair, 2)
    dv, own_resid, vsend, vkeep, wide = call(
        loss_body,
        [
            sds((hrows, width), BF),
            sds((few, width), F32),
            sds((pairs, step, cols), BF),
            sds((pairs, step, cols), F32),
            sds((count + 16, width), BF),
        ],
        [ids, negs, pay_pair, pay_other, normed, rstd, gain, w, w_out, mix, g_block, g_row],
        [pltpu.VMEM((count, width), F32), pltpu.VMEM((width, cols), F32)],
        flops=3 * 10**8,
        moved=6 * 2**20,
    )
    far, near, own, mixed, d_query = call(
        backward_body,
        [
            sds((2, share + few, 2 * width + 128), BF),
            sds((share + few, 2 * width + 128), BF),
            sds((share + few, 2 * width + 128), BF),
            sds((hrows, width), BF),
            sds((count, cols), BF),
        ],
        [ids, hid, w, probs, dv, qk, folded],
        [pltpu.VMEM((hrows, 128), BF), pltpu.VMEM((count, width), BF)],
        flops=10**9,
        moved=8 * 2**20,
    )
    spread = call(
        spread_body,
        [sds((parts, step + 2 * count + 16, cols), BF)],
        [mixed, qx, d_query, cls, wide],
        [pltpu.VMEM((width, cols), F32)],
        flops=10**8,
        moved=3 * 2**20,
    )[0]
    far_got = ent(far, 2)
    pays = [own, ent(near, 1), far_got[0], ent(far_got[1], 1)]
    grad_hidden = call(
        hidden_body,
        [sds((few, seq, width), BF)],
        [*pays, own_resid],
        flops=3 * 10**8,
        moved=4 * 2**20,
    )[0]
    if not direct:
        others = any_size(embed, ctx, spread, vsend, vkeep, wide, table, g_block, g_row, negs)
        return (grad_hidden, *others)

    packed = after(packed, pay_pair)
    zs = jnp.stack([packed, ment(packed, 4)])
    zs = jnp.concatenate([zs, ment(zs, 2)], axis=0)
    tile = (step, cols)
    v_keep, v_sent = call(
        fold_x_body, [sds((2, *tile), F32), sds((2, *tile), BF)], [vkeep, ment(vsend, 1)], moved=2**20
    )
    v_keep, v_send = call(
        fold_z_body, [sds(tile, F32), sds(tile, BF)], [v_keep, ment(v_sent, 2)], moved=2**19
    )
    v_got = ment(v_send, 4)
    gathered = jnp.concatenate([after(zs, v_keep), ment(zs, 1)], axis=0)
    gathered_other = ent(gathered, 1)
    spread = lax.all_to_all(after(spread, v_sent, zs), "ment", 0, 0)
    grad_table = call(
        functools.partial(table_body, negs.shape[0]),
        [sds((blocks, block_rows // parts, width), F32)],
        [ids, gathered, gathered_other, spread, table_rows],
        [pltpu.VMEM((parts * count, blocks * block_rows // parts), BF)],
        flops=5 * 10**8,
        moved=4 * 2**20,
    )[0]
    grad_qkv, grad_wo, grad_ln = call(
        small_body,
        [sds((3, *tile), F32), sds((cols, step), F32), sds((2, step), F32)],
        [ids, gathered, spread, v_keep, v_got],
        flops=10**8,
        moved=2**20,
    )
    return (grad_hidden, jnp.transpose(grad_qkv, (1, 0, 2)), grad_wo, grad_ln, grad_table)


def any_size(embed, ctx, spread, vsend, vkeep, wide, table, g_block, g_row, negs):
    ments = lax.axis_size("ment")
    count, width = embed.shape
    blocks, block_rows = table.shape[0], table.shape[1]
    few_rows = block_rows // ments
    step = width // spread.shape[0]
    sums = wide[count:].astype(F32)
    lse = lax.all_gather(sums[4, :count] + sums[5, :count] + sums[6, :count], "ment")
    blocks_of = lax.all_gather(g_block[0], "ment")
    rows_of = lax.all_gather(g_row[0], "ment")
    lists = lax.all_gather(negs, "ment")
    embeds = lax.all_gather(embed, "ment")
    at = lax.axis_index("ment") * few_rows
    rows = lax.dynamic_slice_in_dim(table, at, few_rows, 1)
    score = jnp.einsum("smd,brd->smbr", embeds, rows, preferred_element_type=F32)
    block = lax.axis_index("ent") * blocks + jnp.arange(blocks, dtype=jnp.int32)
    row = at + jnp.arange(few_rows, dtype=jnp.int32)
    hot = (blocks_of[:, :, None, None] == block[:, None]) & (rows_of[:, :, None, None] == row)
    hot = hot.astype(F32)
    listed = jnp.any(lists[:, :, None] == block, axis=1).astype(F32)
    times = (jnp.sum(hot, axis=1) + listed[:, :, None])[:, None]
    expo = jnp.where(times > 0, times * jnp.exp(score - lse[:, :, None, None]), 0.0)
    grad_table = jnp.einsum("smbr,smd->brd", (expo - hot).astype(BF), embeds, preferred_element_type=F32)
    resid = wide[:count].reshape(count, ments, -1)
    resid = lax.all_to_all(jnp.transpose(resid, (1, 0, 2)), "ment", 0, 0)
    ctxs = lax.all_gather(ctx, "ment")
    grad_wo = jnp.einsum("smc,smd->cd", ctxs, resid, preferred_element_type=F32)
    grad_ln = lax.psum_scatter(sums[0:2] + sums[2:4], "ment", scatter_dimension=1, tiled=True)
    keys = spread[:, :step].astype(F32).reshape(width, -1)
    d_query = spread[0, step : step + count]
    cls = jnp.transpose(spread[:, step + count : step + 2 * count, :step], (1, 0, 2)).reshape(count, width)
    values = jnp.stack([vkeep, vsend.astype(F32)], axis=1).reshape(width, -1)
    whole = jnp.stack([mm_tn(cls, d_query), keys, values], axis=1)
    grad_qkv = lax.psum_scatter(whole, "ment", scatter_dimension=0, tiled=True)
    return grad_qkv, grad_wo, grad_ln, grad_table


def solution(mesh):
    placed = (
        P("ment", None, None),
        P(None, None, "ent"),
        P("ent", None),
        P(),
        P(),
        P("ent", None, None),
        P("ment"),
        P("ment"),
        P("ment"),
        P("ment", None),
    )
    return jax.shard_map(
        on_device,
        mesh=mesh,
        in_specs=placed,
        out_specs=(
            P(("ment", "ent"), None, None),
            P("ment", None, "ent"),
            P("ent", "ment"),
            P(None, "ment"),
            P("ent", "ment", None),
        ),
        check_vma=False,
    )
```

```python
import functools

import jax
import jax.numpy as jnp
from jax import lax
from jax.experimental import pallas as pl
from jax.experimental.pallas import tpu as pltpu
from jax.sharding import PartitionSpec as P

HD = 64
EPS = 1e-06
GROUP = 8
LOW = -1e30
BF = jnp.bfloat16
F32 = jnp.float32
VMEM = pl.BlockSpec(memory_space=pltpu.VMEM)
SMEM = pl.BlockSpec(memory_space=pltpu.SMEM)
HBM = pl.BlockSpec(memory_space=pltpu.HBM)


def mm(a, b):
    return jnp.dot(a, b, preferred_element_type=F32)


def mm_nt(a, b):
    return lax.dot_general(a, b, (((1,), (1,)), ((), ())), preferred_element_type=F32)


def mm_tn(a, b):
    return lax.dot_general(a, b, (((0,), (0,)), ((), ())), preferred_element_type=F32)


def sds(shape, dtype):
    return jax.ShapeDtypeStruct(shape, dtype)


def call(body, outs, ins, scratch=(), flops=0, moved=0, limit=20, outside=0):
    smem = sum(1 for x in ins if x.ndim == 1 and x.dtype == jnp.int32)
    inside = len(ins) - smem - outside
    return pl.pallas_call(
        body,
        out_shape=outs,
        in_specs=[SMEM] * smem + [VMEM] * inside + [HBM] * outside,
        out_specs=[VMEM] * len(outs),
        scratch_shapes=list(scratch),
        compiler_params=pltpu.CompilerParams(vmem_limit_bytes=limit * 2**20),
        cost_estimate=pl.CostEstimate(flops=flops, bytes_accessed=moved, transcendentals=0),
    )(*ins)


def head_mask(heads, cols):
    head = lax.broadcasted_iota(jnp.int32, (1, heads, 1, cols), 1)
    col = lax.broadcasted_iota(jnp.int32, (1, heads, 1, cols), 3)
    return (col // HD == head).astype(F32)


def spread_heads(rows, heads):
    count, cols = rows.shape
    split = rows.reshape(count // GROUP, 1, GROUP, cols)
    return (split * head_mask(heads, cols)).reshape(heads * count, cols).astype(BF)


def pick_heads(rows, heads):
    count, cols = rows.shape
    split = rows.reshape(count // (heads * GROUP), heads, GROUP, cols)
    return jnp.sum(split * head_mask(heads, cols), axis=1).reshape(count // heads, cols)


def forward_body(
    key_len, hid_in, w_in, wo_in, attn, cls_out, ctx_out, probs_out, mix_out, qx_out, qk_out, fold_out,
    hid, w_ref, wo_ref, sems,
):
    tokens, width = hid.shape
    cols = w_ref.shape[2]
    heads = cols // HD
    count = key_len.shape[0]
    seq = tokens // count
    span = GROUP * seq
    rows = GROUP * heads
    groups = count // GROUP
    part = [pltpu.make_async_copy(w_in.at[0], w_ref.at[0], sems.at[groups])]
    part += [
        pltpu.make_async_copy(
            hid_in.at[pl.ds(g * span, span), :], hid.at[pl.ds(g * span, span), :], sems.at[g]
        )
        for g in range(groups)
    ]
    part += [pltpu.make_async_copy(w_in.at[k], w_ref.at[k], sems.at[groups + k]) for k in (1, 2)]
    part += [pltpu.make_async_copy(wo_in, wo_ref, sems.at[groups + 3])]
    for copy in part:
        copy.start()
    line = lax.broadcasted_iota(jnp.int32, (GROUP, width), 0)
    firsts = []
    for g in range(groups):
        part[1 + g].wait()
        rows_of = jnp.zeros((GROUP, width), F32)
        for m in range(GROUP):
            at = g * span + m * seq
            row = hid[at : at + 16, :].astype(F32)[0:1, :]
            rows_of = jnp.where(line == m, row, rows_of)
        firsts.append(rows_of)
    cls = jnp.concatenate(firsts, axis=0).astype(BF)
    cls_out[...] = cls
    part[0].wait()
    query = mm(cls, w_ref[0]).astype(BF).astype(F32)
    qx = spread_heads(query, heads)
    qx_out[...] = qx
    part[groups + 1].wait()
    qk_out[...] = mm_nt(qx, w_ref[1]).astype(BF)
    score = []
    live = []
    col = lax.broadcasted_iota(jnp.int32, (1, span), 1)
    diag = diagonal(rows, span, seq)
    for g in range(groups):
        here = slice(g * rows, (g + 1) * rows)
        score.append(mm_nt(qk_out[here, :], hid[g * span : (g + 1) * span, :]))
        limit = jnp.zeros((1, span), jnp.int32)
        for m in range(GROUP):
            limit = jnp.where(col // seq == m, key_len[g * GROUP + m], limit)
        live.append(jnp.logical_and(diag, col % seq < limit).astype(F32))
    live = jnp.concatenate(live, axis=0) > 0
    score = jnp.where(live, jnp.concatenate(score, axis=0) * HD ** (-0.5), LOW)
    expo = jnp.exp(score - jnp.max(score, axis=1, keepdims=True))
    expo = jnp.where(live, expo, 0.0)
    probs = expo / jnp.sum(expo, axis=1, keepdims=True)
    probs_out[...] = probs
    half = probs.astype(BF)
    for g in range(groups):
        here = slice(g * rows, (g + 1) * rows)
        mix_out[here, :] = mm(half[here, :], hid[g * span : (g + 1) * span, :]).astype(BF)
    fold_out[...] = mm(half, fold_matrix(span, seq, 0)).astype(BF)
    part[groups + 2].wait()
    ctx = pick_heads(mm(mix_out[...], w_ref[2]), heads).astype(BF)
    ctx_out[...] = ctx
    part[groups + 3].wait()
    attn[...] = mm(ctx, wo_ref[...]).astype(BF)


def diagonal(rows, span, seq):
    row = lax.broadcasted_iota(jnp.int32, (rows, span), 0) % GROUP
    return row == lax.broadcasted_iota(jnp.int32, (rows, span), 1) // seq


def fold_matrix(span, seq, at):
    token = lax.broadcasted_iota(jnp.int32, (span, 128), 0) % seq
    lane = lax.broadcasted_iota(jnp.int32, (span, 128), 1)
    return (token + at == lane).astype(F32).astype(BF)


def unfold(lines, rows, span, seq, at):
    token = lax.broadcasted_iota(jnp.int32, (128, span), 1) % seq
    lane = lax.broadcasted_iota(jnp.int32, (128, span), 0)
    wide = mm(lines, (token + at == lane).astype(F32).astype(BF))
    return jnp.where(diagonal(rows, span, seq), wide, 0.0).astype(BF)


def as_column(row):
    n = row.shape[1]
    eye = lax.broadcasted_iota(jnp.int32, (n, n), 0) == lax.broadcasted_iota(jnp.int32, (n, n), 1)
    return jnp.sum(jnp.where(eye, row.astype(F32), 0.0), axis=1, keepdims=True)


def as_row(column):
    n = column.shape[0]
    eye = lax.broadcasted_iota(jnp.int32, (n, n), 0) == lax.broadcasted_iota(jnp.int32, (n, n), 1)
    return jnp.sum(jnp.where(eye, column, 0.0), axis=0, keepdims=True)


def three(x):
    high = x.astype(BF).astype(F32)
    mid = (x - high).astype(BF).astype(F32)
    return high, mid, x - high - mid


def score_body(
    ids, negs, parts, cls, gain, bias, gold_block, gold_row, table, ctx,
    embed_out, normed_out, rstd_out, pay, packed, rows_out, score_buf,
):
    blocks, block_rows, width = table.shape
    count = cls.shape[0]
    half = width // 2
    cols = ctx.shape[1]
    attn = sum(parts[k].astype(F32) for k in range(parts.shape[0]))
    resid = cls[...].astype(F32) + attn
    centre = resid - jnp.mean(resid, axis=1, keepdims=True)
    rstd = lax.rsqrt(jnp.mean(centre * centre, axis=1, keepdims=True) + EPS)
    normed = centre * rstd
    normed_out[...] = normed
    rstd_out[...] = jnp.broadcast_to(rstd, rstd_out.shape)
    embed = (normed * gain[...] + bias[...]).astype(BF)
    embed_out[...] = embed
    first = ids[1] * blocks
    g_block, g_row = as_column(gold_block[...]), as_column(gold_row[...])
    side = ids[1] & 1
    packed[:, 0:half] = embed_out[:, pl.ds(pl.multiple_of(side * half, half), half)]
    packed[:, half : half + cols] = ctx[...]
    tile_rows = rows_out.shape[1]
    rows_out[...] = table[:, pl.ds(pl.multiple_of(ids[0] * tile_rows, tile_rows), tile_rows), :]
    place = (g_block - first.astype(F32)) * block_rows + g_row
    top = jnp.full((count, 1), LOW, F32)
    counts = []
    for b in range(blocks):
        score = mm_nt(embed, table[b])
        score_buf[b] = score
        at = lax.broadcasted_iota(jnp.int32, (count, block_rows), 1) + b * block_rows
        hot = (at.astype(F32) == place).astype(F32)
        times = jnp.sum(hot, axis=0, keepdims=True)
        listed = jnp.int32(0)
        for k in range(negs.shape[0]):
            listed = jnp.where(negs[k] == first + b, 1, listed)
        times = jnp.broadcast_to(times + listed.astype(F32), (count, block_rows))
        top = jnp.maximum(top, jnp.max(jnp.where(times > 0, score, LOW), axis=1, keepdims=True))
        counts.append((times, hot))
    total = jnp.zeros((count, 1), F32)
    mean = jnp.zeros((2 * count, width), F32)
    for b in range(blocks):
        times, hot = counts[b]
        expo = jnp.where(times > 0, times * jnp.exp(jnp.minimum(score_buf[b] - top, 0.0)), 0.0)
        total += jnp.sum(expo, axis=1, keepdims=True)
        mean += mm(jnp.concatenate([expo, hot], axis=0).astype(BF), table[b])
    some = total > 0
    safe = jnp.where(some, total, 1.0)
    store_mean(pay, mean[0:count] / safe, jnp.where(some, top + jnp.log(safe), LOW))
    pay[:, width + 128 :] = mean[count:].astype(BF)


def store_mean(pay, mean, logsum):
    count, width = mean.shape
    pay[:, 0:width] = mean.astype(BF)
    high, mid, low = three(logsum)
    lane = lax.broadcasted_iota(jnp.int32, (count, 128), 1)
    stats = jnp.where(lane == 0, high, jnp.where(lane == 1, mid, jnp.where(lane == 2, low, 0.0)))
    pay[:, width : width + 128] = stats.astype(BF)


def merge_means(p, q, width):
    one, two = [jnp.sum(v[:, width : width + 128].astype(F32), axis=1, keepdims=True) for v in (p, q)]
    top = jnp.maximum(one, two)
    logsum = top + jnp.log(jnp.exp(one - top) + jnp.exp(two - top))
    mean = jnp.exp(one - logsum) * p[:, 0:width].astype(F32)
    golds = p[:, width + 128 :].astype(F32) + q[:, width + 128 :].astype(F32)
    return mean + jnp.exp(two - logsum) * q[:, 0:width].astype(F32), logsum, golds


def merge_body(p, q, out):
    width = (out.shape[1] - 128) // 2
    mean, logsum, golds = merge_means(p[...], q[...], width)
    store_mean(out, mean, logsum)
    out[:, width + 128 :] = golds.astype(BF)


def loss_body(
    ids, negs, p0, p1, normed_ref, rstd_ref, gain, w_ref, wo_ref, mix, gold_block, gold_row,
    dv_out, own_resid, vsend, vkeep, wide, resid_buf, grad_buf,
):
    count, width = normed_ref.shape
    heads = w_ref.shape[2] // HD
    mean, lse, golds = merge_means(p0[...], p1[...], width)
    d_embed = mean - golds
    normed = normed_ref[...]
    upper = d_embed * gain[...]
    d_resid = rstd_ref[:, 0:1] * (
        upper
        - jnp.mean(upper, axis=1, keepdims=True)
        - normed * jnp.mean(upper * normed, axis=1, keepdims=True)
    )
    half = d_resid.astype(BF)
    d_ctx = mm_nt(half, wo_ref[...]).astype(BF).astype(F32)
    dx = spread_heads(d_ctx, heads)
    dv_out[...] = mm_nt(dx, w_ref[2]).astype(BF)
    grad_buf[...] = mm_tn(mix[...], dx)
    store_parts(ids, grad_buf, vsend, vkeep)
    resid_buf[...] = d_resid
    share = own_resid.shape[0]
    own_resid[...] = resid_buf[pl.ds(pl.multiple_of(ids[1] * share, share), share), :]
    first = jnp.sum(d_embed * normed, axis=0, keepdims=True)
    second = jnp.sum(d_embed, axis=0, keepdims=True)
    first_high = first.astype(BF).astype(F32)
    second_high = second.astype(BF).astype(F32)
    lane = lax.broadcasted_iota(jnp.int32, (1, count), 1)
    lists = jnp.zeros((1, count), F32)
    for k in range(negs.shape[0]):
        lists = jnp.where(lane == k, negs[k].astype(F32), lists)
    logs = [*three(as_row(lse)), gold_block[...].astype(F32), gold_row[...].astype(F32), lists]
    logs = [jnp.concatenate([v] * (width // count), axis=1) for v in logs]
    line = lax.broadcasted_iota(jnp.int32, (16, width), 0)
    lines = jnp.zeros((16, width), F32)
    for k, v in enumerate(
        [first_high, second_high, first - first_high, second - second_high] + logs
    ):
        lines = jnp.where(line == k, v, lines)
    wide[0:count, :] = half
    wide[count : count + 16, :] = lines.astype(BF)


def store_parts(ids, grad_buf, send, keep):
    parts = 2 * send.shape[0]
    step = grad_buf.shape[0] // parts
    for d in range(parts):
        part = grad_buf[pl.ds(pl.multiple_of((ids[0] ^ d) * step, step), step), :]
        if d % 2:
            send[d // 2] = part.astype(BF)
        else:
            keep[d // 2] = part


def backward_body(
    ids, hid, w_ref, probs_ref, dv, qk, folded, far, near, own, tbuf, d_query_out, buf, zbuf
):
    tokens, width = hid.shape
    heads = w_ref.shape[2] // HD
    count = d_query_out.shape[0]
    seq = tokens // count
    span = GROUP * seq
    rows = GROUP * heads
    xs = [hid[g * span : (g + 1) * span, :] for g in range(count // GROUP)]
    d_probs = [mm_nt(dv[g * rows : (g + 1) * rows, :], x) for g, x in enumerate(xs)]
    d_probs = jnp.concatenate(d_probs, axis=0)
    probs = probs_ref[...]
    d_scores = probs * (d_probs - jnp.sum(probs * d_probs, axis=1, keepdims=True))
    half = (d_scores * HD ** (-0.5)).astype(BF)
    for g, x in enumerate(xs):
        here = slice(g * rows, (g + 1) * rows)
        tbuf[here, :] = mm(half[here, :], x).astype(BF)
    buf[...] = (folded[...].astype(F32) + mm(half, fold_matrix(span, seq, seq))).astype(BF)
    d_query = pick_heads(mm(tbuf[...], w_ref[1]), heads).astype(BF)
    d_query_out[...] = d_query
    zbuf[...] = mm_nt(d_query, w_ref[0]).astype(BF)
    share = dv.shape[0] // 4
    few = count // 4
    for k, out in ((0, own), (1, near), (2, far.at[0]), (3, far.at[1])):
        peer = ids[1] ^ k
        mine = pl.ds(pl.multiple_of(peer * share, share), share)
        out[0:share, 0:width] = dv[mine, :]
        out[0:share, width : 2 * width] = qk[mine, :]
        out[0:share, 2 * width :] = buf[mine, :]
        out[share : share + few, 0:width] = zbuf[pl.ds(pl.multiple_of(peer * few, few), few), :]
        out[share : share + few, width:] = jnp.zeros((few, width + 128), BF)


def spread_body(tbuf, qx, d_query, cls, wide, spread, grad_buf):
    count, width = cls.shape
    cols = qx.shape[1]
    grad_buf[...] = mm_tn(tbuf[...], qx[...])
    step = width // spread.shape[0]
    at = (step, step + count, step + 2 * count)
    for r in range(spread.shape[0]):
        here = slice(r * step, (r + 1) * step)
        spread[r, 0:step, :] = grad_buf[here, :].astype(BF)
        spread[r, at[0] : at[1], :] = d_query[...]
        spread[r, at[1] : at[2], 0:step] = cls[:, here]
        spread[r, at[1] : at[2], step : 2 * step] = wide[0:count, here]
        spread[r, at[2] :, 0:step] = wide[count:, here]
        spread[r, at[2] :, step:] = jnp.zeros((16, spread.shape[2] - step), BF)


def fold_x_body(keep, got, kept, sent):
    for k in range(2):
        kept[k] = keep[2 * k] + got[2 * k].astype(F32)
        sent[k] = (keep[2 * k + 1] + got[2 * k + 1].astype(F32)).astype(BF)


def fold_z_body(keep, got, kept, sent):
    kept[...] = keep[0] + got[0].astype(F32)
    sent[...] = (keep[1] + got[1].astype(F32)).astype(BF)


def hidden_body(p0, p1, p2, p3, own_resid, out):
    pays = (p0, p1, p2, p3)
    mentions, seq, width = out.shape
    share = p0.shape[0] - mentions
    groups = mentions // GROUP
    rows = share // groups
    span = GROUP * seq
    first = own_resid[...]
    for p in pays:
        first = first + p[share : share + mentions, 0:width].astype(F32)
    token = lax.broadcasted_iota(jnp.int32, (GROUP, seq, width), 1)
    for g in range(groups):
        here = slice(g * rows, (g + 1) * rows)
        left = [unfold(p[here, 2 * width :], rows, span, seq, 0) for p in pays]
        left += [unfold(p[here, 2 * width :], rows, span, seq, seq) for p in pays]
        right = [p[here, 0:width] for p in pays] + [p[here, width : 2 * width] for p in pays]
        grad = mm_tn(jnp.concatenate(left, axis=0), jnp.concatenate(right, axis=0))
        add = first[g * GROUP : (g + 1) * GROUP, :].reshape(GROUP, 1, width)
        grad = grad.reshape(GROUP, seq, width) + jnp.where(token == 0, add, 0.0)
        out[g * GROUP : (g + 1) * GROUP] = grad.astype(BF)


ORDER = (0, 4, 2, 6, 1, 5, 3, 7)


def table_body(listings, ids, mine_all, other_all, spread, rows_ref, out, weights):
    blocks, tile_rows, width = out.shape
    half = width // 2
    count = mine_all.shape[1]
    at = spread.shape[1] - 16
    step = width // spread.shape[0]
    tile = blocks * tile_rows
    side = ids[1] & 1
    mine = pl.ds(pl.multiple_of(side * half, half), half)
    theirs = pl.ds(pl.multiple_of((1 - side) * half, half), half)
    rows_mine = rows_ref[:, :, mine].reshape(tile, half)
    rows_theirs = rows_ref[:, :, theirs].reshape(tile, half)
    sources = [mine_all[k] for k in range(mine_all.shape[0])]
    others = [other_all[k] for k in range(mine_all.shape[0])]
    left = jnp.concatenate([s[:, 0:half] for s in sources], axis=0)
    right = jnp.concatenate([s[:, 0:half] for s in others], axis=0)
    score = mm_nt(left, rows_mine) + mm_nt(right, rows_theirs)
    col = lax.broadcasted_iota(jnp.int32, (1, tile), 1)
    block = (col // tile_rows + ids[1] * blocks).astype(F32)
    row = (col % tile_rows + ids[0] * tile_rows).astype(F32)
    for d, source in enumerate(sources):
        lines = spread[ids[0] ^ ORDER[d], at:, 0:count].astype(F32)
        lse = as_column(lines[4:5] + lines[5:6] + lines[6:7])
        hot = jnp.logical_and(as_column(lines[7:8]) == block, as_column(lines[8:9]) == row).astype(F32)
        times = jnp.sum(hot, axis=0, keepdims=True)
        listed = jnp.zeros((1, tile), F32)
        for k in range(listings):
            listed = jnp.where(lines[9:10, k : k + 1] == block, 1.0, listed)
        times = jnp.broadcast_to(times + listed, (count, tile))
        expo = jnp.exp(score[d * count : (d + 1) * count, :] - lse)
        expo = jnp.where(times > 0, times * expo, 0.0)
        weights[d * count : (d + 1) * count, :] = (expo - hot).astype(BF)
    out[:, :, mine] = mm_tn(weights[...], left).reshape(blocks, tile_rows, half)
    out[:, :, theirs] = mm_tn(weights[...], right).reshape(blocks, tile_rows, half)


def small_body(ids, gathered, spread, v0, v1, qkv_out, wo_out, ln_out):
    cols, step = wo_out.shape
    count = gathered.shape[1]
    at = gathered.shape[2] - cols
    parts = spread.shape[0]
    rows = (step, step + count, step + 2 * count)
    left = [gathered[d, :, at : at + cols] for d in range(parts)]
    right = [spread[ids[0] ^ d, rows[1] : rows[2], step : 2 * step] for d in ORDER]
    wo_out[...] = mm_tn(jnp.concatenate(left, axis=0), jnp.concatenate(right, axis=0))
    total = sum(spread[r, rows[2] :, 0:step].astype(F32) for r in range(parts))
    ln_out[...] = total[0:2, :] + total[2:4, :]
    left = [spread[r, rows[1] : rows[2], 0:step] for r in range(parts)]
    right = [spread[r, rows[0] : rows[1], :] for r in range(parts)]
    qkv_out[0] = mm_tn(jnp.concatenate(left, axis=0), jnp.concatenate(right, axis=0))
    qkv_out[1] = sum(spread[r, 0:step, :].astype(F32) for r in range(parts))
    qkv_out[2] = v0[...] + v1[...].astype(F32)


def swap(x, axis, size, k):
    return lax.ppermute(x, axis, [(i, i ^ k) for i in range(size)])


def after(x, *others):
    return lax.optimization_barrier((x, *others))[0]


def on_device(
    hidden_in, w_qkv, w_out, ln_gain, ln_bias, table, key_len, gold_block, gold_row, neg_blocks
):
    count, seq, width = hidden_in.shape
    cols = w_qkv.shape[2]
    heads = cols // HD
    blocks, block_rows = table.shape[0], table.shape[1]
    ments, ents = lax.axis_size("ment"), lax.axis_size("ent")
    parts = 8
    direct = ments == parts
    mine = lax.axis_index("ment") if direct else 0
    ids = jnp.stack([jnp.int32(mine), lax.axis_index("ent").astype(jnp.int32)])
    hid = hidden_in.reshape(count * seq, width)
    w = jnp.transpose(w_qkv, (1, 0, 2))
    gain, bias = ln_gain.reshape(1, width), ln_bias.reshape(1, width)
    g_block, g_row = gold_block.reshape(1, count), gold_row.reshape(1, count)
    negs = neg_blocks.reshape(neg_blocks.shape[1])
    span = GROUP * seq
    hrows = heads * count
    share = hrows // ents
    few = count // ents
    step = width // parts
    pairs = parts // 2

    def ent(x, k):
        return swap(x, "ent", ents, k)

    def ment(x, k):
        return swap(x, "ment", ments, k)

    attn, cls, ctx, probs, mix, qx, qk, folded = call(
        forward_body,
        [
            sds((count, width), BF),
            sds((count, width), BF),
            sds((count, cols), BF),
            sds((hrows, span), F32),
            sds((hrows, width), BF),
            sds((hrows, cols), BF),
            sds((hrows, width), BF),
            sds((hrows, 128), BF),
        ],
        [key_len, hid, w, w_out],
        [
            pltpu.VMEM(hid.shape, BF),
            pltpu.VMEM(w.shape, BF),
            pltpu.VMEM(w_out.shape, BF),
            pltpu.SemaphoreType.DMA((count // GROUP + 4,)),
        ],
        flops=10**9,
        moved=8 * 2**20,
        limit=52,
        outside=3,
    )
    attns = lax.all_gather(attn, "ent")
    embed, normed, rstd, pay, packed, table_rows = call(
        score_body,
        [
            sds((count, width), BF),
            sds((count, width), F32),
            sds((count, 128), F32),
            sds((count, 2 * width + 128), BF),
            sds((count, width // 2 + cols), BF),
            sds((blocks, block_rows // parts, width), BF),
        ],
        [ids, negs, attns, cls, gain, bias, g_block, g_row, table, ctx],
        [pltpu.VMEM((blocks, count, block_rows), F32)],
        flops=6 * 10**8,
        moved=6 * 2**20,
    )
    pay_pair = call(merge_body, [sds(pay.shape, BF)], [pay, ent(pay, 1)], moved=2**19)[0]
    pay_other = ent(pay_pair, 2)
    dv, own_resid, vsend, vkeep, wide = call(
        loss_body,
        [
            sds((hrows, width), BF),
            sds((few, width), F32),
            sds((pairs, step, cols), BF),
            sds((pairs, step, cols), F32),
            sds((count + 16, width), BF),
        ],
        [ids, negs, pay_pair, pay_other, normed, rstd, gain, w, w_out, mix, g_block, g_row],
        [pltpu.VMEM((count, width), F32), pltpu.VMEM((width, cols), F32)],
        flops=3 * 10**8,
        moved=6 * 2**20,
    )
    far, near, own, mixed, d_query = call(
        backward_body,
        [
            sds((2, share + few, 2 * width + 128), BF),
            sds((share + few, 2 * width + 128), BF),
            sds((share + few, 2 * width + 128), BF),
            sds((hrows, width), BF),
            sds((count, cols), BF),
        ],
        [ids, hid, w, probs, dv, qk, folded],
        [pltpu.VMEM((hrows, 128), BF), pltpu.VMEM((count, width), BF)],
        flops=10**9,
        moved=8 * 2**20,
    )
    spread = call(
        spread_body,
        [sds((parts, step + 2 * count + 16, cols), BF)],
        [mixed, qx, d_query, cls, wide],
        [pltpu.VMEM((width, cols), F32)],
        flops=10**8,
        moved=3 * 2**20,
    )[0]
    far_got = ent(far, 2)
    pays = [own, ent(near, 1), far_got[0], ent(far_got[1], 1)]
    grad_hidden = call(
        hidden_body,
        [sds((few, seq, width), BF)],
        [*pays, own_resid],
        flops=3 * 10**8,
        moved=4 * 2**20,
    )[0]
    if not direct:
        others = any_size(embed, ctx, spread, vsend, vkeep, wide, table, g_block, g_row, negs)
        return (grad_hidden, *others)

    packed = after(packed, pay_pair)
    zs = jnp.stack([packed, ment(packed, 4)])
    zs = jnp.concatenate([zs, ment(zs, 2)], axis=0)
    tile = (step, cols)
    v_keep, v_sent = call(
        fold_x_body, [sds((2, *tile), F32), sds((2, *tile), BF)], [vkeep, ment(vsend, 1)], moved=2**20
    )
    v_keep, v_send = call(
        fold_z_body, [sds(tile, F32), sds(tile, BF)], [v_keep, ment(v_sent, 2)], moved=2**19
    )
    v_got = ment(v_send, 4)
    gathered = jnp.concatenate([after(zs, v_keep), ment(zs, 1)], axis=0)
    gathered_other = ent(gathered, 1)
    spread = lax.all_to_all(after(spread, v_sent, zs), "ment", 0, 0)
    grad_table = call(
        functools.partial(table_body, negs.shape[0]),
        [sds((blocks, block_rows // parts, width), F32)],
        [ids, gathered, gathered_other, spread, table_rows],
        [pltpu.VMEM((parts * count, blocks * block_rows // parts), BF)],
        flops=5 * 10**8,
        moved=4 * 2**20,
    )[0]
    grad_qkv, grad_wo, grad_ln = call(
        small_body,
        [sds((3, *tile), F32), sds((cols, step), F32), sds((2, step), F32)],
        [ids, gathered, after(spread, grad_table), v_keep, v_got],
        flops=10**8,
        moved=2**20,
    )
    return (grad_hidden, jnp.transpose(grad_qkv, (1, 0, 2)), grad_wo, grad_ln, grad_table)


def any_size(embed, ctx, spread, vsend, vkeep, wide, table, g_block, g_row, negs):
    ments = lax.axis_size("ment")
    count, width = embed.shape
    blocks, block_rows = table.shape[0], table.shape[1]
    few_rows = block_rows // ments
    step = width // spread.shape[0]
    sums = wide[count:].astype(F32)
    lse = lax.all_gather(sums[4, :count] + sums[5, :count] + sums[6, :count], "ment")
    blocks_of = lax.all_gather(g_block[0], "ment")
    rows_of = lax.all_gather(g_row[0], "ment")
    lists = lax.all_gather(negs, "ment")
    embeds = lax.all_gather(embed, "ment")
    at = lax.axis_index("ment") * few_rows
    rows = lax.dynamic_slice_in_dim(table, at, few_rows, 1)
    score = jnp.einsum("smd,brd->smbr", embeds, rows, preferred_element_type=F32)
    block = lax.axis_index("ent") * blocks + jnp.arange(blocks, dtype=jnp.int32)
    row = at + jnp.arange(few_rows, dtype=jnp.int32)
    hot = (blocks_of[:, :, None, None] == block[:, None]) & (rows_of[:, :, None, None] == row)
    hot = hot.astype(F32)
    listed = jnp.any(lists[:, :, None] == block, axis=1).astype(F32)
    times = (jnp.sum(hot, axis=1) + listed[:, :, None])[:, None]
    expo = jnp.where(times > 0, times * jnp.exp(score - lse[:, :, None, None]), 0.0)
    grad_table = jnp.einsum("smbr,smd->brd", (expo - hot).astype(BF), embeds, preferred_element_type=F32)
    resid = wide[:count].reshape(count, ments, -1)
    resid = lax.all_to_all(jnp.transpose(resid, (1, 0, 2)), "ment", 0, 0)
    ctxs = lax.all_gather(ctx, "ment")
    grad_wo = jnp.einsum("smc,smd->cd", ctxs, resid, preferred_element_type=F32)
    grad_ln = lax.psum_scatter(sums[0:2] + sums[2:4], "ment", scatter_dimension=1, tiled=True)
    keys = spread[:, :step].astype(F32).reshape(width, -1)
    d_query = spread[0, step : step + count]
    cls = jnp.transpose(spread[:, step + count : step + 2 * count, :step], (1, 0, 2)).reshape(count, width)
    values = jnp.stack([vkeep, vsend.astype(F32)], axis=1).reshape(width, -1)
    whole = jnp.stack([mm_tn(cls, d_query), keys, values], axis=1)
    grad_qkv = lax.psum_scatter(whole, "ment", scatter_dimension=0, tiled=True)
    return grad_qkv, grad_wo, grad_ln, grad_table


def solution(mesh):
    placed = (
        P("ment", None, None),
        P(None, None, "ent"),
        P("ent", None),
        P(),
        P(),
        P("ent", None, None),
        P("ment"),
        P("ment"),
        P("ment"),
        P("ment", None),
    )
    return jax.shard_map(
        on_device,
        mesh=mesh,
        in_specs=placed,
        out_specs=(
            P(("ment", "ent"), None, None),
            P("ment", None, "ent"),
            P("ent", "ment"),
            P(None, "ment"),
            P("ent", "ment", None),
        ),
        check_vma=False,
    )
```

```python
import functools

import jax
import jax.numpy as jnp
from jax import lax
from jax.experimental import pallas as pl
from jax.experimental.pallas import tpu as pltpu
from jax.sharding import PartitionSpec as P

HD = 64
EPS = 1e-06
GROUP = 8
LOW = -1e30
BF = jnp.bfloat16
F32 = jnp.float32
VMEM = pl.BlockSpec(memory_space=pltpu.VMEM)
SMEM = pl.BlockSpec(memory_space=pltpu.SMEM)
HBM = pl.BlockSpec(memory_space=pltpu.HBM)


def mm(a, b):
    return jnp.dot(a, b, preferred_element_type=F32)


def mm_nt(a, b):
    return lax.dot_general(a, b, (((1,), (1,)), ((), ())), preferred_element_type=F32)


def mm_tn(a, b):
    return lax.dot_general(a, b, (((0,), (0,)), ((), ())), preferred_element_type=F32)


def sds(shape, dtype):
    return jax.ShapeDtypeStruct(shape, dtype)


def call(body, outs, ins, scratch=(), flops=0, moved=0, limit=20, outside=0, last=0):
    smem = sum(1 for x in ins if x.ndim == 1 and x.dtype == jnp.int32)
    inside = len(ins) - smem - outside
    return pl.pallas_call(
        body,
        out_shape=outs,
        in_specs=[SMEM] * smem + [VMEM] * inside + [HBM] * outside,
        out_specs=[VMEM] * (len(outs) - last) + [HBM] * last,
        scratch_shapes=list(scratch),
        compiler_params=pltpu.CompilerParams(vmem_limit_bytes=limit * 2**20),
        cost_estimate=pl.CostEstimate(flops=flops, bytes_accessed=moved, transcendentals=0),
    )(*ins)


def head_mask(heads, cols):
    head = lax.broadcasted_iota(jnp.int32, (1, heads, 1, cols), 1)
    col = lax.broadcasted_iota(jnp.int32, (1, heads, 1, cols), 3)
    return (col // HD == head).astype(F32)


def spread_heads(rows, heads):
    count, cols = rows.shape
    split = rows.reshape(count // GROUP, 1, GROUP, cols)
    return (split * head_mask(heads, cols)).reshape(heads * count, cols).astype(BF)


def pick_heads(rows, heads):
    count, cols = rows.shape
    split = rows.reshape(count // (heads * GROUP), heads, GROUP, cols)
    return jnp.sum(split * head_mask(heads, cols), axis=1).reshape(count // heads, cols)


def forward_body(
    key_len, hid_in, w_in, wo_in, attn, cls_out, ctx_out, probs_out, mix_out, qx_out, qk_out, fold_out,
    hid, w_ref, wo_ref, sems,
):
    tokens, width = hid.shape
    cols = w_ref.shape[2]
    heads = cols // HD
    count = key_len.shape[0]
    seq = tokens // count
    span = GROUP * seq
    rows = GROUP * heads
    groups = count // GROUP
    part = [pltpu.make_async_copy(w_in.at[0], w_ref.at[0], sems.at[groups])]
    part += [
        pltpu.make_async_copy(
            hid_in.at[pl.ds(g * span, span), :], hid.at[pl.ds(g * span, span), :], sems.at[g]
        )
        for g in range(groups)
    ]
    part += [pltpu.make_async_copy(w_in.at[k], w_ref.at[k], sems.at[groups + k]) for k in (1, 2)]
    part += [pltpu.make_async_copy(wo_in, wo_ref, sems.at[groups + 3])]
    for copy in part:
        copy.start()
    line = lax.broadcasted_iota(jnp.int32, (GROUP, width), 0)
    firsts = []
    for g in range(groups):
        part[1 + g].wait()
        rows_of = jnp.zeros((GROUP, width), F32)
        for m in range(GROUP):
            at = g * span + m * seq
            row = hid[at : at + 16, :].astype(F32)[0:1, :]
            rows_of = jnp.where(line == m, row, rows_of)
        firsts.append(rows_of)
    cls = jnp.concatenate(firsts, axis=0).astype(BF)
    cls_out[...] = cls
    part[0].wait()
    query = mm(cls, w_ref[0]).astype(BF).astype(F32)
    qx = spread_heads(query, heads)
    qx_out[...] = qx
    part[groups + 1].wait()
    qk_out[...] = mm_nt(qx, w_ref[1]).astype(BF)
    score = []
    live = []
    col = lax.broadcasted_iota(jnp.int32, (1, span), 1)
    diag = diagonal(rows, span, seq)
    for g in range(groups):
        here = slice(g * rows, (g + 1) * rows)
        score.append(mm_nt(qk_out[here, :], hid[g * span : (g + 1) * span, :]))
        limit = jnp.zeros((1, span), jnp.int32)
        for m in range(GROUP):
            limit = jnp.where(col // seq == m, key_len[g * GROUP + m], limit)
        live.append(jnp.logical_and(diag, col % seq < limit).astype(F32))
    live = jnp.concatenate(live, axis=0) > 0
    score = jnp.where(live, jnp.concatenate(score, axis=0) * HD ** (-0.5), LOW)
    expo = jnp.exp(score - jnp.max(score, axis=1, keepdims=True))
    expo = jnp.where(live, expo, 0.0)
    probs = expo / jnp.sum(expo, axis=1, keepdims=True)
    probs_out[...] = probs
    half = probs.astype(BF)
    for g in range(groups):
        here = slice(g * rows, (g + 1) * rows)
        mix_out[here, :] = mm(half[here, :], hid[g * span : (g + 1) * span, :]).astype(BF)
    fold_out[...] = mm(half, fold_matrix(span, seq, 0)).astype(BF)
    part[groups + 2].wait()
    ctx = pick_heads(mm(mix_out[...], w_ref[2]), heads).astype(BF)
    ctx_out[...] = ctx
    part[groups + 3].wait()
    attn[...] = mm(ctx, wo_ref[...]).astype(BF)


def diagonal(rows, span, seq):
    row = lax.broadcasted_iota(jnp.int32, (rows, span), 0) % GROUP
    return row == lax.broadcasted_iota(jnp.int32, (rows, span), 1) // seq


def fold_matrix(span, seq, at):
    token = lax.broadcasted_iota(jnp.int32, (span, 128), 0) % seq
    lane = lax.broadcasted_iota(jnp.int32, (span, 128), 1)
    return (token + at == lane).astype(F32).astype(BF)


def unfold(lines, rows, span, seq, at):
    token = lax.broadcasted_iota(jnp.int32, (128, span), 1) % seq
    lane = lax.broadcasted_iota(jnp.int32, (128, span), 0)
    wide = mm(lines, (token + at == lane).astype(F32).astype(BF))
    return jnp.where(diagonal(rows, span, seq), wide, 0.0).astype(BF)


def as_column(row):
    n = row.shape[1]
    eye = lax.broadcasted_iota(jnp.int32, (n, n), 0) == lax.broadcasted_iota(jnp.int32, (n, n), 1)
    return jnp.sum(jnp.where(eye, row.astype(F32), 0.0), axis=1, keepdims=True)


def as_row(column):
    n = column.shape[0]
    eye = lax.broadcasted_iota(jnp.int32, (n, n), 0) == lax.broadcasted_iota(jnp.int32, (n, n), 1)
    return jnp.sum(jnp.where(eye, column, 0.0), axis=0, keepdims=True)


def three(x):
    high = x.astype(BF).astype(F32)
    mid = (x - high).astype(BF).astype(F32)
    return high, mid, x - high - mid


def score_body(
    ids, negs, parts, cls, gain, bias, gold_block, gold_row, table, ctx,
    embed_out, normed_out, rstd_out, pay, packed, rows_out, score_buf,
):
    blocks, block_rows, width = table.shape
    count = cls.shape[0]
    half = width // 2
    cols = ctx.shape[1]
    attn = sum(parts[k].astype(F32) for k in range(parts.shape[0]))
    resid = cls[...].astype(F32) + attn
    centre = resid - jnp.mean(resid, axis=1, keepdims=True)
    rstd = lax.rsqrt(jnp.mean(centre * centre, axis=1, keepdims=True) + EPS)
    normed = centre * rstd
    normed_out[...] = normed
    rstd_out[...] = jnp.broadcast_to(rstd, rstd_out.shape)
    embed = (normed * gain[...] + bias[...]).astype(BF)
    embed_out[...] = embed
    first = ids[1] * blocks
    g_block, g_row = as_column(gold_block[...]), as_column(gold_row[...])
    side = ids[1] & 1
    packed[:, 0:half] = embed_out[:, pl.ds(pl.multiple_of(side * half, half), half)]
    packed[:, half : half + cols] = ctx[...]
    tile_rows = rows_out.shape[1]
    rows_out[...] = table[:, pl.ds(pl.multiple_of(ids[0] * tile_rows, tile_rows), tile_rows), :]
    place = (g_block - first.astype(F32)) * block_rows + g_row
    top = jnp.full((count, 1), LOW, F32)
    counts = []
    for b in range(blocks):
        score = mm_nt(embed, table[b])
        score_buf[b] = score
        at = lax.broadcasted_iota(jnp.int32, (count, block_rows), 1) + b * block_rows
        hot = (at.astype(F32) == place).astype(F32)
        times = jnp.sum(hot, axis=0, keepdims=True)
        listed = jnp.int32(0)
        for k in range(negs.shape[0]):
            listed = jnp.where(negs[k] == first + b, 1, listed)
        times = jnp.broadcast_to(times + listed.astype(F32), (count, block_rows))
        top = jnp.maximum(top, jnp.max(jnp.where(times > 0, score, LOW), axis=1, keepdims=True))
        counts.append((times, hot))
    total = jnp.zeros((count, 1), F32)
    mean = jnp.zeros((2 * count, width), F32)
    for b in range(blocks):
        times, hot = counts[b]
        expo = jnp.where(times > 0, times * jnp.exp(jnp.minimum(score_buf[b] - top, 0.0)), 0.0)
        total += jnp.sum(expo, axis=1, keepdims=True)
        mean += mm(jnp.concatenate([expo, hot], axis=0).astype(BF), table[b])
    some = total > 0
    safe = jnp.where(some, total, 1.0)
    store_mean(pay, mean[0:count] / safe, jnp.where(some, top + jnp.log(safe), LOW))
    pay[:, width + 128 :] = mean[count:].astype(BF)


def store_mean(pay, mean, logsum):
    count, width = mean.shape
    pay[:, 0:width] = mean.astype(BF)
    high, mid, low = three(logsum)
    lane = lax.broadcasted_iota(jnp.int32, (count, 128), 1)
    stats = jnp.where(lane == 0, high, jnp.where(lane == 1, mid, jnp.where(lane == 2, low, 0.0)))
    pay[:, width : width + 128] = stats.astype(BF)


def merge_means(p, q, width):
    one, two = [jnp.sum(v[:, width : width + 128].astype(F32), axis=1, keepdims=True) for v in (p, q)]
    top = jnp.maximum(one, two)
    logsum = top + jnp.log(jnp.exp(one - top) + jnp.exp(two - top))
    mean = jnp.exp(one - logsum) * p[:, 0:width].astype(F32)
    golds = p[:, width + 128 :].astype(F32) + q[:, width + 128 :].astype(F32)
    return mean + jnp.exp(two - logsum) * q[:, 0:width].astype(F32), logsum, golds


def merge_body(p, q, out):
    width = (out.shape[1] - 128) // 2
    mean, logsum, golds = merge_means(p[...], q[...], width)
    store_mean(out, mean, logsum)
    out[:, width + 128 :] = golds.astype(BF)


def loss_body(
    ids, negs, p0, p1, normed_ref, rstd_ref, gain, w_ref, wo_ref, mix, gold_block, gold_row,
    dx_out, own_resid, vsend, vkeep, wide, resid_buf, grad_buf,
):
    count, width = normed_ref.shape
    heads = w_ref.shape[2] // HD
    mean, lse, golds = merge_means(p0[...], p1[...], width)
    d_embed = mean - golds
    normed = normed_ref[...]
    upper = d_embed * gain[...]
    d_resid = rstd_ref[:, 0:1] * (
        upper
        - jnp.mean(upper, axis=1, keepdims=True)
        - normed * jnp.mean(upper * normed, axis=1, keepdims=True)
    )
    half = d_resid.astype(BF)
    d_ctx = mm_nt(half, wo_ref[...]).astype(BF).astype(F32)
    dx = spread_heads(d_ctx, heads)
    dx_out[...] = dx
    grad_buf[...] = mm_tn(mix[...], dx)
    store_parts(ids, grad_buf, vsend, vkeep)
    resid_buf[...] = d_resid
    share = own_resid.shape[0]
    own_resid[...] = resid_buf[pl.ds(pl.multiple_of(ids[1] * share, share), share), :]
    first = jnp.sum(d_embed * normed, axis=0, keepdims=True)
    second = jnp.sum(d_embed, axis=0, keepdims=True)
    first_high = first.astype(BF).astype(F32)
    second_high = second.astype(BF).astype(F32)
    lane = lax.broadcasted_iota(jnp.int32, (1, count), 1)
    lists = jnp.zeros((1, count), F32)
    for k in range(negs.shape[0]):
        lists = jnp.where(lane == k, negs[k].astype(F32), lists)
    logs = [*three(as_row(lse)), gold_block[...].astype(F32), gold_row[...].astype(F32), lists]
    logs = [jnp.concatenate([v] * (width // count), axis=1) for v in logs]
    line = lax.broadcasted_iota(jnp.int32, (16, width), 0)
    lines = jnp.zeros((16, width), F32)
    for k, v in enumerate(
        [first_high, second_high, first - first_high, second - second_high] + logs
    ):
        lines = jnp.where(line == k, v, lines)
    wide[0:count, :] = half
    wide[count : count + 16, :] = lines.astype(BF)


def store_parts(ids, grad_buf, send, keep):
    parts = 2 * send.shape[0]
    step = grad_buf.shape[0] // parts
    for d in range(parts):
        part = grad_buf[pl.ds(pl.multiple_of((ids[0] ^ d) * step, step), step), :]
        if d % 2:
            send[d // 2] = part.astype(BF)
        else:
            keep[d // 2] = part


def backward_body(
    ids, hid, w_ref, probs_ref, dx, qk, folded, far, near, tbuf, d_query_out, own_out, buf, zbuf, own, dv, sem
):
    dv[...] = mm_nt(dx[...], w_ref[2]).astype(BF)
    tokens, width = hid.shape
    heads = w_ref.shape[2] // HD
    count = d_query_out.shape[0]
    seq = tokens // count
    span = GROUP * seq
    rows = GROUP * heads
    xs = [hid[g * span : (g + 1) * span, :] for g in range(count // GROUP)]
    d_probs = [mm_nt(dv[g * rows : (g + 1) * rows, :], x) for g, x in enumerate(xs)]
    d_probs = jnp.concatenate(d_probs, axis=0)
    probs = probs_ref[...]
    d_scores = probs * (d_probs - jnp.sum(probs * d_probs, axis=1, keepdims=True))
    half = (d_scores * HD ** (-0.5)).astype(BF)
    for g, x in enumerate(xs):
        here = slice(g * rows, (g + 1) * rows)
        tbuf[here, :] = mm(half[here, :], x).astype(BF)
    buf[...] = (folded[...].astype(F32) + mm(half, fold_matrix(span, seq, seq))).astype(BF)
    d_query = pick_heads(mm(tbuf[...], w_ref[1]), heads).astype(BF)
    d_query_out[...] = d_query
    zbuf[...] = mm_nt(d_query, w_ref[0]).astype(BF)
    share = dv.shape[0] // 4
    few = count // 4
    for k, out in ((0, own), (1, near), (2, far.at[0]), (3, far.at[1])):
        peer = ids[1] ^ k
        mine = pl.ds(pl.multiple_of(peer * share, share), share)
        out[0:share, 0:width] = dv[mine, :]
        out[0:share, width : 2 * width] = qk[mine, :]
        out[0:share, 2 * width :] = buf[mine, :]
        out[share : share + few, 0:width] = zbuf[pl.ds(pl.multiple_of(peer * few, few), few), :]
        out[share : share + few, width:] = jnp.zeros((few, width + 128), BF)
        if k == 0:
            store = pltpu.make_async_copy(own, own_out, sem)
            store.start()
    store.wait()


def spread_body(tbuf, qx, d_query, cls, wide, spread, grad_buf):
    count, width = cls.shape
    cols = qx.shape[1]
    grad_buf[...] = mm_tn(tbuf[...], qx[...])
    step = width // spread.shape[0]
    at = (step, step + count, step + 2 * count)
    for r in range(spread.shape[0]):
        here = slice(r * step, (r + 1) * step)
        spread[r, 0:step, :] = grad_buf[here, :].astype(BF)
        spread[r, at[0] : at[1], :] = d_query[...]
        spread[r, at[1] : at[2], 0:step] = cls[:, here]
        spread[r, at[1] : at[2], step : 2 * step] = wide[0:count, here]
        spread[r, at[2] :, 0:step] = wide[count:, here]
        spread[r, at[2] :, step:] = jnp.zeros((16, spread.shape[2] - step), BF)


def fold_x_body(keep, got, kept, sent):
    for k in range(2):
        kept[k] = keep[2 * k] + got[2 * k].astype(F32)
        sent[k] = (keep[2 * k + 1] + got[2 * k + 1].astype(F32)).astype(BF)


def fold_z_body(keep, got, kept, sent):
    kept[...] = keep[0] + got[0].astype(F32)
    sent[...] = (keep[1] + got[1].astype(F32)).astype(BF)


def hidden_body(p0, p1, p2, p3, own_resid, out):
    pays = (p0, p1, p2, p3)
    mentions, seq, width = out.shape
    share = p0.shape[0] - mentions
    groups = mentions // GROUP
    rows = share // groups
    span = GROUP * seq
    first = own_resid[...]
    for p in pays:
        first = first + p[share : share + mentions, 0:width].astype(F32)
    token = lax.broadcasted_iota(jnp.int32, (GROUP, seq, width), 1)
    for g in range(groups):
        here = slice(g * rows, (g + 1) * rows)
        left = [unfold(p[here, 2 * width :], rows, span, seq, 0) for p in pays]
        left += [unfold(p[here, 2 * width :], rows, span, seq, seq) for p in pays]
        right = [p[here, 0:width] for p in pays] + [p[here, width : 2 * width] for p in pays]
        grad = mm_tn(jnp.concatenate(left, axis=0), jnp.concatenate(right, axis=0))
        add = first[g * GROUP : (g + 1) * GROUP, :].reshape(GROUP, 1, width)
        grad = grad.reshape(GROUP, seq, width) + jnp.where(token == 0, add, 0.0)
        out[g * GROUP : (g + 1) * GROUP] = grad.astype(BF)


ORDER = (0, 4, 2, 6, 1, 5, 3, 7)


def table_body(listings, ids, mine_all, other_all, spread, rows_ref, out, weights):
    blocks, tile_rows, width = out.shape
    half = width // 2
    count = mine_all.shape[1]
    at = spread.shape[1] - 16
    step = width // spread.shape[0]
    tile = blocks * tile_rows
    side = ids[1] & 1
    mine = pl.ds(pl.multiple_of(side * half, half), half)
    theirs = pl.ds(pl.multiple_of((1 - side) * half, half), half)
    rows_mine = rows_ref[:, :, mine].reshape(tile, half)
    rows_theirs = rows_ref[:, :, theirs].reshape(tile, half)
    sources = [mine_all[k] for k in range(mine_all.shape[0])]
    others = [other_all[k] for k in range(mine_all.shape[0])]
    left = jnp.concatenate([s[:, 0:half] for s in sources], axis=0)
    right = jnp.concatenate([s[:, 0:half] for s in others], axis=0)
    score = mm_nt(left, rows_mine) + mm_nt(right, rows_theirs)
    col = lax.broadcasted_iota(jnp.int32, (1, tile), 1)
    block = (col // tile_rows + ids[1] * blocks).astype(F32)
    row = (col % tile_rows + ids[0] * tile_rows).astype(F32)
    for d, source in enumerate(sources):
        lines = spread[ids[0] ^ ORDER[d], at:, 0:count].astype(F32)
        lse = as_column(lines[4:5] + lines[5:6] + lines[6:7])
        hot = jnp.logical_and(as_column(lines[7:8]) == block, as_column(lines[8:9]) == row).astype(F32)
        times = jnp.sum(hot, axis=0, keepdims=True)
        listed = jnp.zeros((1, tile), F32)
        for k in range(listings):
            listed = jnp.where(lines[9:10, k : k + 1] == block, 1.0, listed)
        times = jnp.broadcast_to(times + listed, (count, tile))
        expo = jnp.exp(score[d * count : (d + 1) * count, :] - lse)
        expo = jnp.where(times > 0, times * expo, 0.0)
        weights[d * count : (d + 1) * count, :] = (expo - hot).astype(BF)
    out[:, :, mine] = mm_tn(weights[...], left).reshape(blocks, tile_rows, half)
    out[:, :, theirs] = mm_tn(weights[...], right).reshape(blocks, tile_rows, half)


def small_body(ids, gathered, spread, v0, v1, qkv_out, wo_out, ln_out):
    cols, step = wo_out.shape
    count = gathered.shape[1]
    at = gathered.shape[2] - cols
    parts = spread.shape[0]
    rows = (step, step + count, step + 2 * count)
    left = [gathered[d, :, at : at + cols] for d in range(parts)]
    right = [spread[ids[0] ^ d, rows[1] : rows[2], step : 2 * step] for d in ORDER]
    wo_out[...] = mm_tn(jnp.concatenate(left, axis=0), jnp.concatenate(right, axis=0))
    total = sum(spread[r, rows[2] :, 0:step].astype(F32) for r in range(parts))
    ln_out[...] = total[0:2, :] + total[2:4, :]
    left = [spread[r, rows[1] : rows[2], 0:step] for r in range(parts)]
    right = [spread[r, rows[0] : rows[1], :] for r in range(parts)]
    qkv_out[0] = mm_tn(jnp.concatenate(left, axis=0), jnp.concatenate(right, axis=0))
    qkv_out[1] = sum(spread[r, 0:step, :].astype(F32) for r in range(parts))
    qkv_out[2] = v0[...] + v1[...].astype(F32)


def swap(x, axis, size, k):
    return lax.ppermute(x, axis, [(i, i ^ k) for i in range(size)])


def after(x, *others):
    return lax.optimization_barrier((x, *others))[0]


def on_device(
    hidden_in, w_qkv, w_out, ln_gain, ln_bias, table, key_len, gold_block, gold_row, neg_blocks
):
    count, seq, width = hidden_in.shape
    cols = w_qkv.shape[2]
    heads = cols // HD
    blocks, block_rows = table.shape[0], table.shape[1]
    ments, ents = lax.axis_size("ment"), lax.axis_size("ent")
    parts = 8
    direct = ments == parts
    mine = lax.axis_index("ment") if direct else 0
    ids = jnp.stack([jnp.int32(mine), lax.axis_index("ent").astype(jnp.int32)])
    hid = hidden_in.reshape(count * seq, width)
    w = jnp.transpose(w_qkv, (1, 0, 2))
    gain, bias = ln_gain.reshape(1, width), ln_bias.reshape(1, width)
    g_block, g_row = gold_block.reshape(1, count), gold_row.reshape(1, count)
    negs = neg_blocks.reshape(neg_blocks.shape[1])
    span = GROUP * seq
    hrows = heads * count
    share = hrows // ents
    few = count // ents
    step = width // parts
    pairs = parts // 2

    def ent(x, k):
        return swap(x, "ent", ents, k)

    def ment(x, k):
        return swap(x, "ment", ments, k)

    attn, cls, ctx, probs, mix, qx, qk, folded = call(
        forward_body,
        [
            sds((count, width), BF),
            sds((count, width), BF),
            sds((count, cols), BF),
            sds((hrows, span), F32),
            sds((hrows, width), BF),
            sds((hrows, cols), BF),
            sds((hrows, width), BF),
            sds((hrows, 128), BF),
        ],
        [key_len, hid, w, w_out],
        [
            pltpu.VMEM(hid.shape, BF),
            pltpu.VMEM(w.shape, BF),
            pltpu.VMEM(w_out.shape, BF),
            pltpu.SemaphoreType.DMA((count // GROUP + 4,)),
        ],
        flops=10**9,
        moved=8 * 2**20,
        limit=52,
        outside=3,
    )
    attns = lax.all_gather(attn, "ent")
    embed, normed, rstd, pay, packed, table_rows = call(
        score_body,
        [
            sds((count, width), BF),
            sds((count, width), F32),
            sds((count, 128), F32),
            sds((count, 2 * width + 128), BF),
            sds((count, width // 2 + cols), BF),
            sds((blocks, block_rows // parts, width), BF),
        ],
        [ids, negs, attns, cls, gain, bias, g_block, g_row, table, ctx],
        [pltpu.VMEM((blocks, count, block_rows), F32)],
        flops=6 * 10**8,
        moved=6 * 2**20,
    )
    pay_pair = call(merge_body, [sds(pay.shape, BF)], [pay, ent(pay, 1)], moved=2**19)[0]
    pay_other = ent(pay_pair, 2)
    dx, own_resid, vsend, vkeep, wide = call(
        loss_body,
        [
            sds((hrows, cols), BF),
            sds((few, width), F32),
            sds((pairs, step, cols), BF),
            sds((pairs, step, cols), F32),
            sds((count + 16, width), BF),
        ],
        [ids, negs, pay_pair, pay_other, normed, rstd, gain, w, w_out, mix, g_block, g_row],
        [pltpu.VMEM((count, width), F32), pltpu.VMEM((width, cols), F32)],
        flops=3 * 10**8,
        moved=6 * 2**20,
    )
    far, near, mixed, d_query, own = call(
        backward_body,
        [
            sds((2, share + few, 2 * width + 128), BF),
            sds((share + few, 2 * width + 128), BF),
            sds((hrows, width), BF),
            sds((count, cols), BF),
            sds((share + few, 2 * width + 128), BF),
        ],
        [ids, hid, w, probs, dx, qk, folded],
        [
            pltpu.VMEM((hrows, 128), BF),
            pltpu.VMEM((count, width), BF),
            pltpu.VMEM((share + few, 2 * width + 128), BF),
            pltpu.VMEM((hrows, width), BF),
            pltpu.SemaphoreType.DMA,
        ],
        last=1,
        flops=10**9,
        moved=8 * 2**20,
    )
    spread = call(
        spread_body,
        [sds((parts, step + 2 * count + 16, cols), BF)],
        [mixed, qx, d_query, cls, wide],
        [pltpu.VMEM((width, cols), F32)],
        flops=10**8,
        moved=3 * 2**20,
    )[0]
    far_got = ent(far, 2)
    pays = [own, ent(near, 1), far_got[0], ent(far_got[1], 1)]
    grad_hidden = call(
        hidden_body,
        [sds((few, seq, width), BF)],
        [*pays, own_resid],
        flops=3 * 10**8,
        moved=4 * 2**20,
    )[0]
    if not direct:
        others = any_size(embed, ctx, spread, vsend, vkeep, wide, table, g_block, g_row, negs)
        return (grad_hidden, *others)

    packed = after(packed, pay_pair)
    zs = jnp.stack([packed, ment(packed, 4)])
    zs = jnp.concatenate([zs, ment(zs, 2)], axis=0)
    tile = (step, cols)
    v_keep, v_sent = call(
        fold_x_body, [sds((2, *tile), F32), sds((2, *tile), BF)], [vkeep, ment(vsend, 1)], moved=2**20
    )
    v_keep, v_send = call(
        fold_z_body, [sds(tile, F32), sds(tile, BF)], [v_keep, ment(v_sent, 2)], moved=2**19
    )
    v_got = ment(v_send, 4)
    gathered = jnp.concatenate([after(zs, v_keep), ment(zs, 1)], axis=0)
    gathered_other = ent(gathered, 1)
    spread = lax.all_to_all(after(spread, v_sent, zs), "ment", 0, 0)
    grad_table = call(
        functools.partial(table_body, negs.shape[0]),
        [sds((blocks, block_rows // parts, width), F32)],
        [ids, gathered, gathered_other, spread, table_rows],
        [pltpu.VMEM((parts * count, blocks * block_rows // parts), BF)],
        flops=5 * 10**8,
        moved=4 * 2**20,
    )[0]
    grad_qkv, grad_wo, grad_ln = call(
        small_body,
        [sds((3, *tile), F32), sds((cols, step), F32), sds((2, step), F32)],
        [ids, gathered, after(spread, grad_table), v_keep, v_got],
        flops=10**8,
        moved=2**20,
    )
    return (grad_hidden, jnp.transpose(grad_qkv, (1, 0, 2)), grad_wo, grad_ln, grad_table)


def any_size(embed, ctx, spread, vsend, vkeep, wide, table, g_block, g_row, negs):
    ments = lax.axis_size("ment")
    count, width = embed.shape
    blocks, block_rows = table.shape[0], table.shape[1]
    few_rows = block_rows // ments
    step = width // spread.shape[0]
    sums = wide[count:].astype(F32)
    lse = lax.all_gather(sums[4, :count] + sums[5, :count] + sums[6, :count], "ment")
    blocks_of = lax.all_gather(g_block[0], "ment")
    rows_of = lax.all_gather(g_row[0], "ment")
    lists = lax.all_gather(negs, "ment")
    embeds = lax.all_gather(embed, "ment")
    at = lax.axis_index("ment") * few_rows
    rows = lax.dynamic_slice_in_dim(table, at, few_rows, 1)
    score = jnp.einsum("smd,brd->smbr", embeds, rows, preferred_element_type=F32)
    block = lax.axis_index("ent") * blocks + jnp.arange(blocks, dtype=jnp.int32)
    row = at + jnp.arange(few_rows, dtype=jnp.int32)
    hot = (blocks_of[:, :, None, None] == block[:, None]) & (rows_of[:, :, None, None] == row)
    hot = hot.astype(F32)
    listed = jnp.any(lists[:, :, None] == block, axis=1).astype(F32)
    times = (jnp.sum(hot, axis=1) + listed[:, :, None])[:, None]
    expo = jnp.where(times > 0, times * jnp.exp(score - lse[:, :, None, None]), 0.0)
    grad_table = jnp.einsum("smbr,smd->brd", (expo - hot).astype(BF), embeds, preferred_element_type=F32)
    resid = wide[:count].reshape(count, ments, -1)
    resid = lax.all_to_all(jnp.transpose(resid, (1, 0, 2)), "ment", 0, 0)
    ctxs = lax.all_gather(ctx, "ment")
    grad_wo = jnp.einsum("smc,smd->cd", ctxs, resid, preferred_element_type=F32)
    grad_ln = lax.psum_scatter(sums[0:2] + sums[2:4], "ment", scatter_dimension=1, tiled=True)
    keys = spread[:, :step].astype(F32).reshape(width, -1)
    d_query = spread[0, step : step + count]
    cls = jnp.transpose(spread[:, step + count : step + 2 * count, :step], (1, 0, 2)).reshape(count, width)
    values = jnp.stack([vkeep, vsend.astype(F32)], axis=1).reshape(width, -1)
    whole = jnp.stack([mm_tn(cls, d_query), keys, values], axis=1)
    grad_qkv = lax.psum_scatter(whole, "ment", scatter_dimension=0, tiled=True)
    return grad_qkv, grad_wo, grad_ln, grad_table


def solution(mesh):
    placed = (
        P("ment", None, None),
        P(None, None, "ent"),
        P("ent", None),
        P(),
        P(),
        P("ent", None, None),
        P("ment"),
        P("ment"),
        P("ment"),
        P("ment", None),
    )
    return jax.shard_map(
        on_device,
        mesh=mesh,
        in_specs=placed,
        out_specs=(
            P(("ment", "ent"), None, None),
            P("ment", None, "ent"),
            P("ent", "ment"),
            P(None, "ment"),
            P("ent", "ment", None),
        ),
        check_vma=False,
    )
```

```python
import functools

import jax
import jax.numpy as jnp
from jax import lax
from jax.experimental import pallas as pl
from jax.experimental.pallas import tpu as pltpu
from jax.sharding import PartitionSpec as P

HD = 64
EPS = 1e-06
GROUP = 8
LOW = -1e30
BF = jnp.bfloat16
F32 = jnp.float32
VMEM = pl.BlockSpec(memory_space=pltpu.VMEM)
SMEM = pl.BlockSpec(memory_space=pltpu.SMEM)
HBM = pl.BlockSpec(memory_space=pltpu.HBM)


def mm(a, b):
    return jnp.dot(a, b, preferred_element_type=F32)


def mm_nt(a, b):
    return lax.dot_general(a, b, (((1,), (1,)), ((), ())), preferred_element_type=F32)


def mm_tn(a, b):
    return lax.dot_general(a, b, (((0,), (0,)), ((), ())), preferred_element_type=F32)


def sds(shape, dtype):
    return jax.ShapeDtypeStruct(shape, dtype)


def call(body, outs, ins, scratch=(), flops=0, moved=0, limit=20, outside=0, last=0):
    smem = sum(1 for x in ins[: len(ins) - outside] if x.ndim == 1 and x.dtype == jnp.int32)
    inside = len(ins) - smem - outside
    return pl.pallas_call(
        body,
        out_shape=outs,
        in_specs=[SMEM] * smem + [VMEM] * inside + [HBM] * outside,
        out_specs=[VMEM] * (len(outs) - last) + [HBM] * last,
        scratch_shapes=list(scratch),
        compiler_params=pltpu.CompilerParams(vmem_limit_bytes=limit * 2**20),
        cost_estimate=pl.CostEstimate(flops=flops, bytes_accessed=moved, transcendentals=0),
    )(*ins)


def head_mask(heads, cols):
    head = lax.broadcasted_iota(jnp.int32, (1, heads, 1, cols), 1)
    col = lax.broadcasted_iota(jnp.int32, (1, heads, 1, cols), 3)
    return (col // HD == head).astype(F32)


def spread_heads(rows, heads):
    count, cols = rows.shape
    split = rows.reshape(count // GROUP, 1, GROUP, cols)
    return (split * head_mask(heads, cols)).reshape(heads * count, cols).astype(BF)


def pick_heads(rows, heads):
    count, cols = rows.shape
    split = rows.reshape(count // (heads * GROUP), heads, GROUP, cols)
    return jnp.sum(split * head_mask(heads, cols), axis=1).reshape(count // heads, cols)


def forward_body(
    hid_in, w_in, wo_in, key_in, attn, cls_out, ctx_out, probs_out, mix_out, qx_out, qk_out, fold_out,
    hid, w_ref, wo_ref, key_len, sems,
):
    tokens, width = hid.shape
    cols = w_ref.shape[2]
    heads = cols // HD
    count = key_len.shape[0]
    seq = tokens // count
    span = GROUP * seq
    rows = GROUP * heads
    groups = count // GROUP
    part = [pltpu.make_async_copy(w_in.at[0], w_ref.at[0], sems.at[groups])]
    part += [
        pltpu.make_async_copy(
            hid_in.at[pl.ds(g * span, span), :], hid.at[pl.ds(g * span, span), :], sems.at[g]
        )
        for g in range(groups)
    ]
    part += [pltpu.make_async_copy(w_in.at[k], w_ref.at[k], sems.at[groups + k]) for k in (1, 2)]
    part += [pltpu.make_async_copy(wo_in, wo_ref, sems.at[groups + 3])]
    part += [pltpu.make_async_copy(key_in, key_len, sems.at[groups + 4])]
    for copy in part:
        copy.start()
    line = lax.broadcasted_iota(jnp.int32, (GROUP, width), 0)
    firsts = []
    for g in range(groups):
        part[1 + g].wait()
        rows_of = jnp.zeros((GROUP, width), F32)
        for m in range(GROUP):
            at = g * span + m * seq
            row = hid[at : at + 16, :].astype(F32)[0:1, :]
            rows_of = jnp.where(line == m, row, rows_of)
        firsts.append(rows_of)
    cls = jnp.concatenate(firsts, axis=0).astype(BF)
    cls_out[...] = cls
    part[0].wait()
    query = mm(cls, w_ref[0]).astype(BF).astype(F32)
    qx = spread_heads(query, heads)
    qx_out[...] = qx
    part[groups + 1].wait()
    qk_out[...] = mm_nt(qx, w_ref[1]).astype(BF)
    part[groups + 4].wait()
    score = []
    live = []
    col = lax.broadcasted_iota(jnp.int32, (1, span), 1)
    diag = diagonal(rows, span, seq)
    for g in range(groups):
        here = slice(g * rows, (g + 1) * rows)
        score.append(mm_nt(qk_out[here, :], hid[g * span : (g + 1) * span, :]))
        limit = jnp.zeros((1, span), jnp.int32)
        for m in range(GROUP):
            limit = jnp.where(col // seq == m, key_len[g * GROUP + m], limit)
        live.append(jnp.logical_and(diag, col % seq < limit).astype(F32))
    live = jnp.concatenate(live, axis=0) > 0
    score = jnp.where(live, jnp.concatenate(score, axis=0) * HD ** (-0.5), LOW)
    expo = jnp.exp(score - jnp.max(score, axis=1, keepdims=True))
    expo = jnp.where(live, expo, 0.0)
    probs = expo / jnp.sum(expo, axis=1, keepdims=True)
    probs_out[...] = probs
    half = probs.astype(BF)
    for g in range(groups):
        here = slice(g * rows, (g + 1) * rows)
        mix_out[here, :] = mm(half[here, :], hid[g * span : (g + 1) * span, :]).astype(BF)
    fold_out[...] = mm(half, fold_matrix(span, seq, 0)).astype(BF)
    part[groups + 2].wait()
    ctx = pick_heads(mm(mix_out[...], w_ref[2]), heads).astype(BF)
    ctx_out[...] = ctx
    part[groups + 3].wait()
    attn[...] = mm(ctx, wo_ref[...]).astype(BF)


def diagonal(rows, span, seq):
    row = lax.broadcasted_iota(jnp.int32, (rows, span), 0) % GROUP
    return row == lax.broadcasted_iota(jnp.int32, (rows, span), 1) // seq


def fold_matrix(span, seq, at):
    token = lax.broadcasted_iota(jnp.int32, (span, 128), 0) % seq
    lane = lax.broadcasted_iota(jnp.int32, (span, 128), 1)
    return (token + at == lane).astype(F32).astype(BF)


def unfold(lines, rows, span, seq, at):
    token = lax.broadcasted_iota(jnp.int32, (128, span), 1) % seq
    lane = lax.broadcasted_iota(jnp.int32, (128, span), 0)
    wide = mm(lines, (token + at == lane).astype(F32).astype(BF))
    return jnp.where(diagonal(rows, span, seq), wide, 0.0).astype(BF)


def as_column(row):
    n = row.shape[1]
    eye = lax.broadcasted_iota(jnp.int32, (n, n), 0) == lax.broadcasted_iota(jnp.int32, (n, n), 1)
    return jnp.sum(jnp.where(eye, row.astype(F32), 0.0), axis=1, keepdims=True)


def as_row(column):
    n = column.shape[0]
    eye = lax.broadcasted_iota(jnp.int32, (n, n), 0) == lax.broadcasted_iota(jnp.int32, (n, n), 1)
    return jnp.sum(jnp.where(eye, column, 0.0), axis=0, keepdims=True)


def three(x):
    high = x.astype(BF).astype(F32)
    mid = (x - high).astype(BF).astype(F32)
    return high, mid, x - high - mid


def score_body(
    ids, negs, parts, cls, gain, bias, gold_block, gold_row, table, ctx,
    embed_out, normed_out, rstd_out, pay, packed, rows_out, score_buf,
):
    blocks, block_rows, width = table.shape
    count = cls.shape[0]
    half = width // 2
    cols = ctx.shape[1]
    attn = sum(parts[k].astype(F32) for k in range(parts.shape[0]))
    resid = cls[...].astype(F32) + attn
    centre = resid - jnp.mean(resid, axis=1, keepdims=True)
    rstd = lax.rsqrt(jnp.mean(centre * centre, axis=1, keepdims=True) + EPS)
    normed = centre * rstd
    normed_out[...] = normed
    rstd_out[...] = jnp.broadcast_to(rstd, rstd_out.shape)
    embed = (normed * gain[...] + bias[...]).astype(BF)
    embed_out[...] = embed
    first = ids[1] * blocks
    g_block, g_row = as_column(gold_block[...]), as_column(gold_row[...])
    side = ids[1] & 1
    packed[:, 0:half] = embed_out[:, pl.ds(pl.multiple_of(side * half, half), half)]
    packed[:, half : half + cols] = ctx[...]
    tile_rows = rows_out.shape[1]
    rows_out[...] = table[:, pl.ds(pl.multiple_of(ids[0] * tile_rows, tile_rows), tile_rows), :]
    place = (g_block - first.astype(F32)) * block_rows + g_row
    top = jnp.full((count, 1), LOW, F32)
    counts = []
    for b in range(blocks):
        score = mm_nt(embed, table[b])
        score_buf[b] = score
        at = lax.broadcasted_iota(jnp.int32, (count, block_rows), 1) + b * block_rows
        hot = (at.astype(F32) == place).astype(F32)
        times = jnp.sum(hot, axis=0, keepdims=True)
        listed = jnp.int32(0)
        for k in range(negs.shape[0]):
            listed = jnp.where(negs[k] == first + b, 1, listed)
        times = jnp.broadcast_to(times + listed.astype(F32), (count, block_rows))
        top = jnp.maximum(top, jnp.max(jnp.where(times > 0, score, LOW), axis=1, keepdims=True))
        counts.append((times, hot))
    total = jnp.zeros((count, 1), F32)
    mean = jnp.zeros((2 * count, width), F32)
    for b in range(blocks):
        times, hot = counts[b]
        expo = jnp.where(times > 0, times * jnp.exp(jnp.minimum(score_buf[b] - top, 0.0)), 0.0)
        total += jnp.sum(expo, axis=1, keepdims=True)
        mean += mm(jnp.concatenate([expo, hot], axis=0).astype(BF), table[b])
    some = total > 0
    safe = jnp.where(some, total, 1.0)
    store_mean(pay, mean[0:count] / safe, jnp.where(some, top + jnp.log(safe), LOW))
    pay[:, width + 128 :] = mean[count:].astype(BF)


def store_mean(pay, mean, logsum):
    count, width = mean.shape
    pay[:, 0:width] = mean.astype(BF)
    high, mid, low = three(logsum)
    lane = lax.broadcasted_iota(jnp.int32, (count, 128), 1)
    stats = jnp.where(lane == 0, high, jnp.where(lane == 1, mid, jnp.where(lane == 2, low, 0.0)))
    pay[:, width : width + 128] = stats.astype(BF)


def merge_means(p, q, width):
    one, two = [jnp.sum(v[:, width : width + 128].astype(F32), axis=1, keepdims=True) for v in (p, q)]
    top = jnp.maximum(one, two)
    logsum = top + jnp.log(jnp.exp(one - top) + jnp.exp(two - top))
    mean = jnp.exp(one - logsum) * p[:, 0:width].astype(F32)
    golds = p[:, width + 128 :].astype(F32) + q[:, width + 128 :].astype(F32)
    return mean + jnp.exp(two - logsum) * q[:, 0:width].astype(F32), logsum, golds


def merge_body(p, q, out):
    width = (out.shape[1] - 128) // 2
    mean, logsum, golds = merge_means(p[...], q[...], width)
    store_mean(out, mean, logsum)
    out[:, width + 128 :] = golds.astype(BF)


def loss_body(
    ids, negs, p0, p1, normed_ref, rstd_ref, gain, w_ref, wo_ref, mix, gold_block, gold_row,
    dx_out, own_resid, vsend, vkeep, wide, resid_buf, grad_buf,
):
    count, width = normed_ref.shape
    heads = w_ref.shape[2] // HD
    mean, lse, golds = merge_means(p0[...], p1[...], width)
    d_embed = mean - golds
    normed = normed_ref[...]
    upper = d_embed * gain[...]
    d_resid = rstd_ref[:, 0:1] * (
        upper
        - jnp.mean(upper, axis=1, keepdims=True)
        - normed * jnp.mean(upper * normed, axis=1, keepdims=True)
    )
    half = d_resid.astype(BF)
    d_ctx = mm_nt(half, wo_ref[...]).astype(BF).astype(F32)
    dx = spread_heads(d_ctx, heads)
    dx_out[...] = dx
    grad_buf[...] = mm_tn(mix[...], dx)
    store_parts(ids, grad_buf, vsend, vkeep)
    resid_buf[...] = d_resid
    share = own_resid.shape[0]
    own_resid[...] = resid_buf[pl.ds(pl.multiple_of(ids[1] * share, share), share), :]
    first = jnp.sum(d_embed * normed, axis=0, keepdims=True)
    second = jnp.sum(d_embed, axis=0, keepdims=True)
    first_high = first.astype(BF).astype(F32)
    second_high = second.astype(BF).astype(F32)
    lane = lax.broadcasted_iota(jnp.int32, (1, count), 1)
    lists = jnp.zeros((1, count), F32)
    for k in range(negs.shape[0]):
        lists = jnp.where(lane == k, negs[k].astype(F32), lists)
    logs = [*three(as_row(lse)), gold_block[...].astype(F32), gold_row[...].astype(F32), lists]
    logs = [jnp.concatenate([v] * (width // count), axis=1) for v in logs]
    line = lax.broadcasted_iota(jnp.int32, (16, width), 0)
    lines = jnp.zeros((16, width), F32)
    for k, v in enumerate(
        [first_high, second_high, first - first_high, second - second_high] + logs
    ):
        lines = jnp.where(line == k, v, lines)
    wide[0:count, :] = half
    wide[count : count + 16, :] = lines.astype(BF)


def store_parts(ids, grad_buf, send, keep):
    parts = 2 * send.shape[0]
    step = grad_buf.shape[0] // parts
    for d in range(parts):
        part = grad_buf[pl.ds(pl.multiple_of((ids[0] ^ d) * step, step), step), :]
        if d % 2:
            send[d // 2] = part.astype(BF)
        else:
            keep[d // 2] = part


def backward_body(
    ids, hid, w_ref, probs_ref, dx, qk, folded, far, near, tbuf, d_query_out, own_out, buf, zbuf, own, dv, sem
):
    dv[...] = mm_nt(dx[...], w_ref[2]).astype(BF)
    tokens, width = hid.shape
    heads = w_ref.shape[2] // HD
    count = d_query_out.shape[0]
    seq = tokens // count
    span = GROUP * seq
    rows = GROUP * heads
    xs = [hid[g * span : (g + 1) * span, :] for g in range(count // GROUP)]
    d_probs = [mm_nt(dv[g * rows : (g + 1) * rows, :], x) for g, x in enumerate(xs)]
    d_probs = jnp.concatenate(d_probs, axis=0)
    probs = probs_ref[...]
    d_scores = probs * (d_probs - jnp.sum(probs * d_probs, axis=1, keepdims=True))
    half = (d_scores * HD ** (-0.5)).astype(BF)
    for g, x in enumerate(xs):
        here = slice(g * rows, (g + 1) * rows)
        tbuf[here, :] = mm(half[here, :], x).astype(BF)
    buf[...] = (folded[...].astype(F32) + mm(half, fold_matrix(span, seq, seq))).astype(BF)
    d_query = pick_heads(mm(tbuf[...], w_ref[1]), heads).astype(BF)
    d_query_out[...] = d_query
    zbuf[...] = mm_nt(d_query, w_ref[0]).astype(BF)
    share = dv.shape[0] // 4
    few = count // 4
    for k, out in ((0, own), (1, near), (2, far.at[0]), (3, far.at[1])):
        peer = ids[1] ^ k
        mine = pl.ds(pl.multiple_of(peer * share, share), share)
        out[0:share, 0:width] = dv[mine, :]
        out[0:share, width : 2 * width] = qk[mine, :]
        out[0:share, 2 * width :] = buf[mine, :]
        out[share : share + few, 0:width] = zbuf[pl.ds(pl.multiple_of(peer * few, few), few), :]
        out[share : share + few, width:] = jnp.zeros((few, width + 128), BF)
        if k == 0:
            store = pltpu.make_async_copy(own, own_out, sem)
            store.start()
    store.wait()


def spread_body(tbuf, qx, d_query, cls, wide, spread, grad_buf):
    count, width = cls.shape
    cols = qx.shape[1]
    grad_buf[...] = mm_tn(tbuf[...], qx[...])
    step = width // spread.shape[0]
    at = (step, step + count, step + 2 * count)
    for r in range(spread.shape[0]):
        here = slice(r * step, (r + 1) * step)
        spread[r, 0:step, :] = grad_buf[here, :].astype(BF)
        spread[r, at[0] : at[1], :] = d_query[...]
        spread[r, at[1] : at[2], 0:step] = cls[:, here]
        spread[r, at[1] : at[2], step : 2 * step] = wide[0:count, here]
        spread[r, at[2] :, 0:step] = wide[count:, here]
        spread[r, at[2] :, step:] = jnp.zeros((16, spread.shape[2] - step), BF)


def fold_x_body(keep, got, kept, sent):
    for k in range(2):
        kept[k] = keep[2 * k] + got[2 * k].astype(F32)
        sent[k] = (keep[2 * k + 1] + got[2 * k + 1].astype(F32)).astype(BF)


def fold_z_body(keep, got, kept, sent):
    kept[...] = keep[0] + got[0].astype(F32)
    sent[...] = (keep[1] + got[1].astype(F32)).astype(BF)


def hidden_body(p0, p1, p2, p3, own_resid, out):
    pays = (p0, p1, p2, p3)
    mentions, seq, width = out.shape
    share = p0.shape[0] - mentions
    groups = mentions // GROUP
    rows = share // groups
    span = GROUP * seq
    first = own_resid[...]
    for p in pays:
        first = first + p[share : share + mentions, 0:width].astype(F32)
    token = lax.broadcasted_iota(jnp.int32, (GROUP, seq, width), 1)
    for g in range(groups):
        here = slice(g * rows, (g + 1) * rows)
        left = [unfold(p[here, 2 * width :], rows, span, seq, 0) for p in pays]
        left += [unfold(p[here, 2 * width :], rows, span, seq, seq) for p in pays]
        right = [p[here, 0:width] for p in pays] + [p[here, width : 2 * width] for p in pays]
        grad = mm_tn(jnp.concatenate(left, axis=0), jnp.concatenate(right, axis=0))
        add = first[g * GROUP : (g + 1) * GROUP, :].reshape(GROUP, 1, width)
        grad = grad.reshape(GROUP, seq, width) + jnp.where(token == 0, add, 0.0)
        out[g * GROUP : (g + 1) * GROUP] = grad.astype(BF)


ORDER = (0, 4, 2, 6, 1, 5, 3, 7)


def table_body(listings, ids, mine_all, other_all, spread, rows_ref, out, weights):
    blocks, tile_rows, width = out.shape
    half = width // 2
    count = mine_all.shape[1]
    at = spread.shape[1] - 16
    step = width // spread.shape[0]
    tile = blocks * tile_rows
    side = ids[1] & 1
    mine = pl.ds(pl.multiple_of(side * half, half), half)
    theirs = pl.ds(pl.multiple_of((1 - side) * half, half), half)
    rows_mine = rows_ref[:, :, mine].reshape(tile, half)
    rows_theirs = rows_ref[:, :, theirs].reshape(tile, half)
    sources = [mine_all[k] for k in range(mine_all.shape[0])]
    others = [other_all[k] for k in range(mine_all.shape[0])]
    left = jnp.concatenate([s[:, 0:half] for s in sources], axis=0)
    right = jnp.concatenate([s[:, 0:half] for s in others], axis=0)
    score = mm_nt(left, rows_mine) + mm_nt(right, rows_theirs)
    col = lax.broadcasted_iota(jnp.int32, (1, tile), 1)
    block = (col // tile_rows + ids[1] * blocks).astype(F32)
    row = (col % tile_rows + ids[0] * tile_rows).astype(F32)
    for d, source in enumerate(sources):
        lines = spread[ids[0] ^ ORDER[d], at:, 0:count].astype(F32)
        lse = as_column(lines[4:5] + lines[5:6] + lines[6:7])
        hot = jnp.logical_and(as_column(lines[7:8]) == block, as_column(lines[8:9]) == row).astype(F32)
        times = jnp.sum(hot, axis=0, keepdims=True)
        listed = jnp.zeros((1, tile), F32)
        for k in range(listings):
            listed = jnp.where(lines[9:10, k : k + 1] == block, 1.0, listed)
        times = jnp.broadcast_to(times + listed, (count, tile))
        expo = jnp.exp(score[d * count : (d + 1) * count, :] - lse)
        expo = jnp.where(times > 0, times * expo, 0.0)
        weights[d * count : (d + 1) * count, :] = (expo - hot).astype(BF)
    out[:, :, mine] = mm_tn(weights[...], left).reshape(blocks, tile_rows, half)
    out[:, :, theirs] = mm_tn(weights[...], right).reshape(blocks, tile_rows, half)


def small_body(ids, gathered, spread, v0, v1, qkv_out, wo_out, ln_out):
    cols, step = wo_out.shape
    count = gathered.shape[1]
    at = gathered.shape[2] - cols
    parts = spread.shape[0]
    rows = (step, step + count, step + 2 * count)
    left = [gathered[d, :, at : at + cols] for d in range(parts)]
    right = [spread[ids[0] ^ d, rows[1] : rows[2], step : 2 * step] for d in ORDER]
    wo_out[...] = mm_tn(jnp.concatenate(left, axis=0), jnp.concatenate(right, axis=0))
    total = sum(spread[r, rows[2] :, 0:step].astype(F32) for r in range(parts))
    ln_out[...] = total[0:2, :] + total[2:4, :]
    left = [spread[r, rows[1] : rows[2], 0:step] for r in range(parts)]
    right = [spread[r, rows[0] : rows[1], :] for r in range(parts)]
    qkv_out[0] = mm_tn(jnp.concatenate(left, axis=0), jnp.concatenate(right, axis=0))
    qkv_out[1] = sum(spread[r, 0:step, :].astype(F32) for r in range(parts))
    qkv_out[2] = v0[...] + v1[...].astype(F32)


def swap(x, axis, size, k):
    return lax.ppermute(x, axis, [(i, i ^ k) for i in range(size)])


def after(x, *others):
    return lax.optimization_barrier((x, *others))[0]


def on_device(
    hidden_in, w_qkv, w_out, ln_gain, ln_bias, table, key_len, gold_block, gold_row, neg_blocks
):
    count, seq, width = hidden_in.shape
    cols = w_qkv.shape[2]
    heads = cols // HD
    blocks, block_rows = table.shape[0], table.shape[1]
    ments, ents = lax.axis_size("ment"), lax.axis_size("ent")
    parts = 8
    direct = ments == parts
    mine = lax.axis_index("ment") if direct else 0
    ids = jnp.stack([jnp.int32(mine), lax.axis_index("ent").astype(jnp.int32)])
    hid = hidden_in.reshape(count * seq, width)
    w = jnp.transpose(w_qkv, (1, 0, 2))
    gain, bias = ln_gain.reshape(1, width), ln_bias.reshape(1, width)
    g_block, g_row = gold_block.reshape(1, count), gold_row.reshape(1, count)
    negs = neg_blocks.reshape(neg_blocks.shape[1])
    span = GROUP * seq
    hrows = heads * count
    share = hrows // ents
    few = count // ents
    step = width // parts
    pairs = parts // 2

    def ent(x, k):
        return swap(x, "ent", ents, k)

    def ment(x, k):
        return swap(x, "ment", ments, k)

    attn, cls, ctx, probs, mix, qx, qk, folded = call(
        forward_body,
        [
            sds((count, width), BF),
            sds((count, width), BF),
            sds((count, cols), BF),
            sds((hrows, span), F32),
            sds((hrows, width), BF),
            sds((hrows, cols), BF),
            sds((hrows, width), BF),
            sds((hrows, 128), BF),
        ],
        [hid, w, w_out, key_len],
        [
            pltpu.VMEM(hid.shape, BF),
            pltpu.VMEM(w.shape, BF),
            pltpu.VMEM(w_out.shape, BF),
            pltpu.SMEM(key_len.shape, jnp.int32),
            pltpu.SemaphoreType.DMA((count // GROUP + 5,)),
        ],
        flops=10**9,
        moved=8 * 2**20,
        limit=52,
        outside=4,
    )
    attns = lax.all_gather(attn, "ent")
    embed, normed, rstd, pay, packed, table_rows = call(
        score_body,
        [
            sds((count, width), BF),
            sds((count, width), F32),
            sds((count, 128), F32),
            sds((count, 2 * width + 128), BF),
            sds((count, width // 2 + cols), BF),
            sds((blocks, block_rows // parts, width), BF),
        ],
        [ids, negs, attns, cls, gain, bias, g_block, g_row, table, ctx],
        [pltpu.VMEM((blocks, count, block_rows), F32)],
        flops=6 * 10**8,
        moved=6 * 2**20,
    )
    pay_pair = call(merge_body, [sds(pay.shape, BF)], [pay, ent(pay, 1)], moved=2**19)[0]
    pay_other = ent(pay_pair, 2)
    dx, own_resid, vsend, vkeep, wide = call(
        loss_body,
        [
            sds((hrows, cols), BF),
            sds((few, width), F32),
            sds((pairs, step, cols), BF),
            sds((pairs, step, cols), F32),
            sds((count + 16, width), BF),
        ],
        [ids, negs, pay_pair, pay_other, normed, rstd, gain, w, w_out, mix, g_block, g_row],
        [pltpu.VMEM((count, width), F32), pltpu.VMEM((width, cols), F32)],
        flops=3 * 10**8,
        moved=6 * 2**20,
    )
    far, near, mixed, d_query, own = call(
        backward_body,
        [
            sds((2, share + few, 2 * width + 128), BF),
            sds((share + few, 2 * width + 128), BF),
            sds((hrows, width), BF),
            sds((count, cols), BF),
            sds((share + few, 2 * width + 128), BF),
        ],
        [ids, hid, w, probs, dx, qk, folded],
        [
            pltpu.VMEM((hrows, 128), BF),
            pltpu.VMEM((count, width), BF),
            pltpu.VMEM((share + few, 2 * width + 128), BF),
            pltpu.VMEM((hrows, width), BF),
            pltpu.SemaphoreType.DMA,
        ],
        last=1,
        flops=10**9,
        moved=8 * 2**20,
    )
    spread = call(
        spread_body,
        [sds((parts, step + 2 * count + 16, cols), BF)],
        [mixed, qx, d_query, cls, wide],
        [pltpu.VMEM((width, cols), F32)],
        flops=10**8,
        moved=3 * 2**20,
    )[0]
    far_got = ent(far, 2)
    pays = [own, ent(near, 1), far_got[0], ent(far_got[1], 1)]
    grad_hidden = call(
        hidden_body,
        [sds((few, seq, width), BF)],
        [*pays, own_resid],
        flops=3 * 10**8,
        moved=4 * 2**20,
    )[0]
    if not direct:
        others = any_size(embed, ctx, spread, vsend, vkeep, wide, table, g_block, g_row, negs)
        return (grad_hidden, *others)

    packed = after(packed, pay_pair)
    zs = jnp.stack([packed, ment(packed, 4)])
    zs = jnp.concatenate([zs, ment(zs, 2)], axis=0)
    tile = (step, cols)
    v_keep, v_sent = call(
        fold_x_body, [sds((2, *tile), F32), sds((2, *tile), BF)], [vkeep, ment(vsend, 1)], moved=2**20
    )
    v_keep, v_send = call(
        fold_z_body, [sds(tile, F32), sds(tile, BF)], [v_keep, ment(v_sent, 2)], moved=2**19
    )
    v_got = ment(v_send, 4)
    gathered = jnp.concatenate([zs, ment(zs, 1)], axis=0)
    gathered_other = ent(after(gathered, v_keep), 1)
    spread = lax.all_to_all(after(spread, v_sent, zs), "ment", 0, 0)
    grad_table = call(
        functools.partial(table_body, negs.shape[0]),
        [sds((blocks, block_rows // parts, width), F32)],
        [ids, gathered, gathered_other, spread, table_rows],
        [pltpu.VMEM((parts * count, blocks * block_rows // parts), BF)],
        flops=5 * 10**8,
        moved=4 * 2**20,
    )[0]
    grad_qkv, grad_wo, grad_ln = call(
        small_body,
        [sds((3, *tile), F32), sds((cols, step), F32), sds((2, step), F32)],
        [ids, gathered, after(spread, grad_table), v_keep, v_got],
        flops=10**8,
        moved=2**20,
    )
    return (grad_hidden, jnp.transpose(grad_qkv, (1, 0, 2)), grad_wo, grad_ln, grad_table)


def any_size(embed, ctx, spread, vsend, vkeep, wide, table, g_block, g_row, negs):
    ments = lax.axis_size("ment")
    count, width = embed.shape
    blocks, block_rows = table.shape[0], table.shape[1]
    few_rows = block_rows // ments
    step = width // spread.shape[0]
    sums = wide[count:].astype(F32)
    lse = lax.all_gather(sums[4, :count] + sums[5, :count] + sums[6, :count], "ment")
    blocks_of = lax.all_gather(g_block[0], "ment")
    rows_of = lax.all_gather(g_row[0], "ment")
    lists = lax.all_gather(negs, "ment")
    embeds = lax.all_gather(embed, "ment")
    at = lax.axis_index("ment") * few_rows
    rows = lax.dynamic_slice_in_dim(table, at, few_rows, 1)
    score = jnp.einsum("smd,brd->smbr", embeds, rows, preferred_element_type=F32)
    block = lax.axis_index("ent") * blocks + jnp.arange(blocks, dtype=jnp.int32)
    row = at + jnp.arange(few_rows, dtype=jnp.int32)
    hot = (blocks_of[:, :, None, None] == block[:, None]) & (rows_of[:, :, None, None] == row)
    hot = hot.astype(F32)
    listed = jnp.any(lists[:, :, None] == block, axis=1).astype(F32)
    times = (jnp.sum(hot, axis=1) + listed[:, :, None])[:, None]
    expo = jnp.where(times > 0, times * jnp.exp(score - lse[:, :, None, None]), 0.0)
    grad_table = jnp.einsum("smbr,smd->brd", (expo - hot).astype(BF), embeds, preferred_element_type=F32)
    resid = wide[:count].reshape(count, ments, -1)
    resid = lax.all_to_all(jnp.transpose(resid, (1, 0, 2)), "ment", 0, 0)
    ctxs = lax.all_gather(ctx, "ment")
    grad_wo = jnp.einsum("smc,smd->cd", ctxs, resid, preferred_element_type=F32)
    grad_ln = lax.psum_scatter(sums[0:2] + sums[2:4], "ment", scatter_dimension=1, tiled=True)
    keys = spread[:, :step].astype(F32).reshape(width, -1)
    d_query = spread[0, step : step + count]
    cls = jnp.transpose(spread[:, step + count : step + 2 * count, :step], (1, 0, 2)).reshape(count, width)
    values = jnp.stack([vkeep, vsend.astype(F32)], axis=1).reshape(width, -1)
    whole = jnp.stack([mm_tn(cls, d_query), keys, values], axis=1)
    grad_qkv = lax.psum_scatter(whole, "ment", scatter_dimension=0, tiled=True)
    return grad_qkv, grad_wo, grad_ln, grad_table


def solution(mesh):
    placed = (
        P("ment", None, None),
        P(None, None, "ent"),
        P("ent", None),
        P(),
        P(),
        P("ent", None, None),
        P("ment"),
        P("ment"),
        P("ment"),
        P("ment", None),
    )
    return jax.shard_map(
        on_device,
        mesh=mesh,
        in_specs=placed,
        out_specs=(
            P(("ment", "ent"), None, None),
            P("ment", None, "ent"),
            P("ent", "ment"),
            P(None, "ment"),
            P("ent", "ment", None),
        ),
        check_vma=False,
    )
```
